256 devices in a mesh: fsdp: 32 (over x, y, core), tensor: 8 (over z).
Axes of the slice: x: 4, y: 4, z: 8, core: 2. Of those that a mesh axis runs over, the one named last changes fastest.
Arguments:
- weight: bfloat16 [8192, 26624], P('fsdp', 'tensor'), may hold values from -6 to 6
- momentum: bfloat16 [8192, 26624], P('fsdp', 'tensor'), may hold values from -80 to 80
- grad: bfloat16 [8192, 26624], P('fsdp', 'tensor'), may hold values from -80 to 80
- q_factor: bfloat16 [26624, 256], P('tensor'), may hold values from -6 to 6
Outputs:
- new_weight: bfloat16 [8192, 26624], P('fsdp', 'tensor')
- new_momentum: bfloat16 [8192, 26624], P('fsdp', 'tensor')
- new_factor: bfloat16 [26624, 256], P('tensor')
The draws below stay inside these ranges and needn't reach their ends.
All inputs are finite; a program needn't handle non-finite values.
Results may differ from the reference program's by a relative error of at most 0.012.
Values may be sent and summed in bfloat16 or wider, within the bound.
No kernel may reach another device: no remote copies, remote signals or barrier semaphores. Data moves between devices by JAX's collectives and lax.ppermute only.
A program may use at most 64 MiB of HBM per device.

```python
import math
import jax
import jax.numpy as jnp
from jax import lax

D = 8192
FF = 26624
RANK = 256


def common_scales(key):
    row_key = jax.random.fold_in(key, 101)
    col_key = jax.random.fold_in(key, 102)
    row_scale = 10.0 ** jax.random.uniform(row_key, (D,), jnp.float32)
    row_scale = row_scale * (1.0 + 2.0 * jnp.arange(D, dtype=jnp.float32) / (D - 1))
    col_scale = 10.0 ** jax.random.uniform(col_key, (FF,), jnp.float32)
    col_scale = col_scale * (1.0 + 2.0 * jnp.arange(FF, dtype=jnp.float32) / (FF - 1))
    return 0.02 * row_scale[:, None] * col_scale[None, :]


def draw_momentum(key, part):
    scales = common_scales(key)
    key = jax.random.fold_in(key, 7)
    values = jnp.clip(jax.random.normal(key, (D, FF), jnp.float32), -4.0, 4.0)
    return (values * scales).astype(jnp.bfloat16)


def draw_grad(key, part):
    scales = common_scales(key)
    key = jax.random.fold_in(key, 11)
    values = jnp.clip(jax.random.normal(key, (D, FF), jnp.float32), -4.0, 4.0)
    return (values * scales).astype(jnp.bfloat16)


def block_scale(stream_key, extent, pieces, smallest, top_value):
    loudness, own = 1.0, jax.random.fold_in(stream_key, 6)
    for position, shards_of in pieces:
        steps = jnp.exp(jax.random.uniform(jax.random.fold_in(own, position), (shards_of,), jnp.float32, smallest / len(pieces), top_value / len(pieces)))
        loudness = loudness * jnp.repeat(steps, extent[position] // shards_of).reshape([-1 if axis == position else 1 for axis in range(len(extent))])
    return loudness


def centred(key, extent, scale, bound, shards=(), kind=jnp.bfloat16):
    level = block_scale(key, extent, shards, -0.22, 0.18) if shards else 1.0
    drawn = jax.random.normal(key, extent, jnp.float32) * scale * level
    return jnp.minimum(jnp.maximum(drawn, -bound), bound).astype(kind)


def setup_inputs(seed: int = 0) -> dict:
    keys = jax.random.split(jax.random.key(seed), 5)
    weight = centred(keys[0], (D, FF), 1.0, 6.0, ((0, 32), (1, 8)))
    momentum = draw_momentum(jax.random.fold_in(keys[4], 71), 0)
    grad = draw_grad(jax.random.fold_in(keys[4], 71), 0)
    q_factor = centred(keys[3], (FF, RANK), 1.0, 6.0, ((0, 8),))
    return {"weight": weight, "momentum": momentum, "grad": grad, "q_factor": q_factor}


epsilon = 1e-06
keep_rate = 0.9
step_rate = 0.5

def inverse_rms(squares, entries):
    return lax.rsqrt(squares / entries + epsilon)

def orthonormal(rows, triangle):
    solved = jax.scipy.linalg.solve_triangular(triangle, rows.T, lower=True).T
    return (math.sqrt(D) * solved).astype(jnp.bfloat16)

def reference(weight, momentum, grad, q_factor):
    buffer = (momentum.astype(jnp.float32) + grad.astype(jnp.float32)).astype(jnp.bfloat16)
    products = jnp.dot(buffer.astype(jnp.float32), q_factor.astype(jnp.float32), preferred_element_type=jnp.float32)
    gram_total = lax.dot_general(products.astype(jnp.float32), products.astype(jnp.float32), (((0,), (0,)), ((), ())), precision=lax.Precision.HIGHEST, preferred_element_type=jnp.float32)
    triangle = jnp.linalg.cholesky(gram_total)
    left_factor = orthonormal(products, triangle)
    col_factor = jnp.dot(buffer.T.astype(jnp.float32), left_factor.astype(jnp.float32), preferred_element_type=jnp.float32)
    squares = lax.optimization_barrier(jnp.sum(col_factor * col_factor, axis=0))
    new_factor = (col_factor * inverse_rms(squares, FF)).astype(jnp.bfloat16)
    scaled = (left_factor.astype(jnp.float32) * jnp.sqrt(squares / FF + epsilon)).astype(jnp.bfloat16)
    feedback = jnp.dot(scaled.astype(jnp.float32), new_factor.T.astype(jnp.float32), preferred_element_type=jnp.float32)
    new_momentum = (buffer.astype(jnp.float32) - (1.0 - keep_rate) / D * feedback).astype(jnp.bfloat16)
    update = jnp.dot(left_factor.astype(jnp.float32), new_factor.T.astype(jnp.float32), preferred_element_type=jnp.float32)
    new_weight = (weight.astype(jnp.float32) - step_rate / math.sqrt(RANK) * update).astype(jnp.bfloat16)
    return (new_weight, new_momentum, new_factor)
```

```python
import math

import jax
import jax.numpy as jnp
from jax import lax
from jax.experimental import pallas as pl
from jax.experimental.pallas import tpu as pltpu
from jax.sharding import Mesh, PartitionSpec as P

D = 8192
FF = 26624
RANK = 256

epsilon = 1e-06
keep_rate = 0.9
step_rate = 0.5

HIGHEST = lax.Precision.HIGHEST
f32 = jnp.float32
bf16 = jnp.bfloat16

CORE = "core"
PLANE = ("x", "y")
DEPTH = "z"
EVERY = ("x", "y", "core", "z")


def exact_dot(a, b, contract):
    dims = (((contract[0],), (contract[1],)), ((), ()))
    return lax.dot_general(a, b, dims, precision=HIGHEST, preferred_element_type=f32)


LEAF = 64
PANEL = 16


def leaf_inverse(a):
    n = a.shape[0]
    lanes = 2 * n
    rows = lax.broadcasted_iota(jnp.int32, (n, n), 0)
    cols = lax.broadcasted_iota(jnp.int32, (n, n), 1)
    eye = (rows == cols).astype(f32)
    both = jnp.concatenate([a, eye], axis=1)
    count = n // 8
    slabs = [both[8 * i : 8 * i + 8, :] for i in range(count)]
    row8 = lax.broadcasted_iota(jnp.int32, (8, lanes), 0)
    for first in range(0, count, PANEL // 8):
        panel = [
            [
                jnp.broadcast_to(slabs[i][:, 8 * first + k : 8 * first + k + 1], (8, lanes))
                for i in range(first, count)
            ]
            for k in range(PANEL)
        ]
        for k in range(PANEL):
            at, sub = first + k // 8, k % 8
            pivot = jnp.broadcast_to(panel[k][at - first][sub : sub + 1, :], (8, lanes))
            inverse = 1.0 / pivot
            factor = {}
            for i in range(at, count):
                value = panel[k][i - first] * inverse
                factor[i] = jnp.where(row8 > sub, value, 0.0) if i == at else value
            for m in range(k + 1, PANEL):
                row = jnp.broadcast_to(panel[m][at - first][sub : sub + 1, :], (8, lanes))
                for i in range(at, count):
                    panel[m][i - first] = panel[m][i - first] - factor[i] * row
            row = jnp.broadcast_to(slabs[at][sub : sub + 1, :], (8, lanes))
            for i in range(at, count):
                slabs[i] = slabs[i] - factor[i] * row
    both = jnp.concatenate(slabs, axis=0)
    pivots = jnp.sum(both[:, :n] * eye, axis=1, keepdims=True)
    return both[:, n:] * lax.rsqrt(pivots)


def triangle_inverse(a):
    n = a.shape[0]
    if n <= LEAF:
        return leaf_inverse(a)
    h = n // 2
    upper = triangle_inverse(a[:h, :h])
    below = exact_dot(a[h:, :h], upper, (1, 1))
    rest = a[h:, h:] - exact_dot(below, below, (1, 1))
    mixed = exact_dot(below, upper, (1, 0))
    lower = triangle_inverse(rest)
    corner = -exact_dot(lower, mixed, (1, 0))
    top = jnp.concatenate([upper, jnp.zeros((h, n - h), f32)], axis=1)
    return jnp.concatenate([top, jnp.concatenate([corner, lower], axis=1)], axis=0)


def cholesky_inverse(gram):
    def kernel(gram_ref, inverse_ref):
        inverse_ref[...] = triangle_inverse(gram_ref[...])

    return pl.pallas_call(
        kernel,
        out_shape=jax.ShapeDtypeStruct((RANK, RANK), f32),
        in_specs=[pl.BlockSpec(memory_space=pltpu.VMEM)],
        out_specs=pl.BlockSpec(memory_space=pltpu.VMEM),
        compiler_params=pltpu.CompilerParams(vmem_limit_bytes=32 * 2**20),
    )(gram)


def scatter_sum(value, axis, parts):
    pieces = value.reshape(parts, value.shape[0] // parts, *value.shape[1:])
    got = lax.all_to_all(pieces, axis, 0, 0)
    return jnp.sum(got.astype(f32), axis=0)


def gather(value, axis, parts):
    copies = jnp.broadcast_to(value[None], (parts, *value.shape))
    return lax.all_to_all(copies, axis, 0, 0)


def swap_core(value):
    return lax.ppermute(value, CORE, [(0, 1), (1, 0)])


def ring_sum(value, axis, size):
    total = value
    for step in range(1, size):
        total = total + lax.ppermute(
            value, axis, [(i, (i + step) % size) for i in range(size)]
        )
    return total


def sum_fsdp(value):
    core = lax.axis_index(CORE)
    half = value.shape[0] // 2
    value = value + swap_core(value)
    mine = lax.dynamic_slice_in_dim(value, core * half, half, 0)
    mine = ring_sum(mine, "x", 4)
    mine = ring_sum(mine, "y", 4)
    other = swap_core(mine)
    first = core == 0
    return jnp.concatenate([jnp.where(first, mine, other), jnp.where(first, other, mine)], axis=0)


def on_device(weight, momentum, grad, q_factor):
    core = lax.axis_index(CORE)
    buffer = (momentum.astype(f32) + grad.astype(f32)).astype(bf16)
    partial_value = jnp.dot(buffer, q_factor, preferred_element_type=f32)
    products = gather(scatter_sum(partial_value, DEPTH, 8), DEPTH, 8).reshape(256, RANK)
    gram = sum_fsdp(exact_dot(products, products, (0, 0)))
    inverse = cholesky_inverse(gram)
    left_factor = (math.sqrt(D) * exact_dot(products, inverse, (1, 1))).astype(bf16)

    col_partial = lax.dot_general(
        buffer, left_factor, (((0,), (0,)), ((), ())), preferred_element_type=f32
    )
    half = col_partial.shape[0] // 2
    mine = lax.dynamic_slice_in_dim(col_partial, core * half, half, 0)
    theirs = lax.dynamic_slice_in_dim(col_partial, (1 - core) * half, half, 0)
    mine = mine + swap_core(theirs.astype(bf16)).astype(f32)
    share = scatter_sum(mine.astype(bf16), PLANE, 16)

    squares = jnp.sum(gather(jnp.sum(share * share, axis=0)[None], EVERY, 256), axis=(0, 1))
    normalized = (share * lax.rsqrt(squares / FF + epsilon)).astype(bf16)
    mine = gather(normalized, PLANE, 16).reshape(half, RANK)
    other = swap_core(mine)
    first = core == 0
    new_factor = jnp.concatenate(
        [jnp.where(first, mine, other), jnp.where(first, other, mine)], axis=0
    )

    scaled = (left_factor.astype(f32) * jnp.sqrt(squares / FF + epsilon)).astype(bf16)
    feedback = lax.dot_general(
        scaled, new_factor, (((1,), (1,)), ((), ())), preferred_element_type=f32
    )
    new_momentum = (buffer.astype(f32) - (1.0 - keep_rate) / D * feedback).astype(bf16)
    update = lax.dot_general(
        left_factor, new_factor, (((1,), (1,)), ((), ())), preferred_element_type=f32
    )
    new_weight = (weight.astype(f32) - step_rate / math.sqrt(RANK) * update).astype(bf16)
    return (new_weight, new_momentum, new_factor)


def solution(mesh):
    fine = Mesh(mesh.devices.reshape(4, 4, 2, 8), EVERY)
    rows = ("x", "y", CORE)
    placed = (P(rows, DEPTH), P(rows, DEPTH), P(rows, DEPTH), P(DEPTH, None))
    return jax.shard_map(
        on_device,
        mesh=fine,
        in_specs=placed,
        out_specs=(P(rows, DEPTH), P(rows, DEPTH), P(DEPTH, None)),
        check_vma=False,
    )
```

```python
import math

import jax
import jax.numpy as jnp
from jax import lax
from jax.experimental import pallas as pl
from jax.experimental.pallas import tpu as pltpu
from jax.sharding import Mesh, PartitionSpec as P

D = 8192
FF = 26624
RANK = 256

epsilon = 1e-06
keep_rate = 0.9
step_rate = 0.5

HIGHEST = lax.Precision.HIGHEST
f32 = jnp.float32
bf16 = jnp.bfloat16

CORE = "core"
PLANE = ("x", "y")
DEPTH = "z"
EVERY = ("x", "y", "core", "z")

ROWS = 256
COLS = 3328
HALF = 1664
PEERS = 16
SHARE = 104
GRAM = 8
PACK = 128
DEPTHS = 8
LIMIT = 4.0


def exact_dot(a, b, contract):
    dims = (((contract[0],), (contract[1],)), ((), ()))
    return lax.dot_general(a, b, dims, precision=HIGHEST, preferred_element_type=f32)


def plain_dot(a, b, contract):
    dims = (((contract[0],), (contract[1],)), ((), ()))
    return lax.dot_general(a, b, dims, preferred_element_type=f32)


def in_vmem(count):
    return [pl.BlockSpec(memory_space=pltpu.VMEM)] * count


SCALAR = pl.BlockSpec(memory_space=pltpu.SMEM)
PARAMS = pltpu.CompilerParams(vmem_limit_bytes=20 * 2**20)


LEAF = 64
PANEL = 16


def leaf_inverse(a):
    n = a.shape[0]
    lanes = 2 * n
    rows = lax.broadcasted_iota(jnp.int32, (n, n), 0)
    cols = lax.broadcasted_iota(jnp.int32, (n, n), 1)
    eye = (rows == cols).astype(f32)
    both = jnp.concatenate([a, eye], axis=1)
    count = n // 8
    slabs = [both[8 * i : 8 * i + 8, :] for i in range(count)]
    row8 = lax.broadcasted_iota(jnp.int32, (8, lanes), 0)
    for first in range(0, count, PANEL // 8):
        panel = [
            [
                jnp.broadcast_to(slabs[i][:, 8 * first + k : 8 * first + k + 1], (8, lanes))
                for i in range(first, count)
            ]
            for k in range(PANEL)
        ]
        for k in range(PANEL):
            at, sub = first + k // 8, k % 8
            pivot = jnp.broadcast_to(panel[k][at - first][sub : sub + 1, :], (8, lanes))
            inverse = 1.0 / pivot
            factor = {}
            for i in range(at, count):
                value = panel[k][i - first] * inverse
                factor[i] = jnp.where(row8 > sub, value, 0.0) if i == at else value
            for m in range(k + 1, PANEL):
                row = jnp.broadcast_to(panel[m][at - first][sub : sub + 1, :], (8, lanes))
                for i in range(at, count):
                    panel[m][i - first] = panel[m][i - first] - factor[i] * row
            row = jnp.broadcast_to(slabs[at][sub : sub + 1, :], (8, lanes))
            for i in range(at, count):
                slabs[i] = slabs[i] - factor[i] * row
    both = jnp.concatenate(slabs, axis=0)
    pivots = jnp.sum(both[:, :n] * eye, axis=1, keepdims=True)
    return both[:, n:] * lax.rsqrt(pivots)


def triangle_inverse(a):
    n = a.shape[0]
    if n <= LEAF:
        return leaf_inverse(a)
    h = n // 2
    upper = triangle_inverse(a[:h, :h])
    below = exact_dot(a[h:, :h], upper, (1, 1))
    rest = a[h:, h:] - exact_dot(below, below, (1, 1))
    mixed = exact_dot(below, upper, (1, 0))
    lower = triangle_inverse(rest)
    corner = -exact_dot(lower, mixed, (1, 0))
    top = jnp.concatenate([upper, jnp.zeros((h, n - h), f32)], axis=1)
    return jnp.concatenate([top, jnp.concatenate([corner, lower], axis=1)], axis=0)


def cholesky_inverse(gram):
    def kernel(gram_ref, inverse_ref):
        inverse_ref[...] = triangle_inverse(gram_ref[...])

    return pl.pallas_call(
        kernel,
        out_shape=jax.ShapeDtypeStruct((RANK, RANK), f32),
        in_specs=in_vmem(1),
        out_specs=in_vmem(1)[0],
        compiler_params=PARAMS,
    )(gram)


def exchange(pieces, axis):
    return lax.all_to_all(pieces, axis, 0, 0)


def scatter_sum(value, axis, parts):
    pieces = value.reshape(parts, value.shape[0] // parts, *value.shape[1:])
    return jnp.sum(exchange(pieces, axis).astype(f32), axis=0)


def gather(value, axis, parts):
    return exchange(jnp.broadcast_to(value[None], (parts, *value.shape)), axis)


def swap_core(value):
    return lax.ppermute(value, CORE, [(0, 1), (1, 0)])


def in_order(core, mine, other):
    first = core == 0
    return jnp.concatenate([jnp.where(first, mine, other), jnp.where(first, other, mine)], axis=0)


def guarded(total, energy, rows):
    size = jnp.sum(total[:rows] * total[:rows], axis=0, keepdims=True)
    growth = jnp.sum(energy / size, axis=1, keepdims=True) * (1.0 / RANK)
    return jnp.where(growth <= LIMIT, total, jnp.nan)


def split(value):
    high = value.astype(bf16).astype(f32)
    rest = value - high
    middle = rest.astype(bf16).astype(f32)
    return high, middle, rest - middle


def sum_products(parts):
    def kernel(parts_ref, out_ref):
        total = jnp.zeros((ROWS // DEPTHS, RANK), f32)
        energy = jnp.zeros((1, RANK), f32)
        for i in range(DEPTHS):
            part = parts_ref[i].astype(f32)
            total = total + part
            energy = energy + jnp.sum(part * part, axis=0, keepdims=True)
        total = guarded(total, energy, ROWS // DEPTHS).astype(bf16)
        for i in range(DEPTHS):
            out_ref[i] = total

    return pl.pallas_call(
        kernel,
        out_shape=jax.ShapeDtypeStruct(parts.shape, bf16),
        in_specs=in_vmem(1),
        out_specs=in_vmem(1)[0],
        compiler_params=PARAMS,
    )(parts)


def first_shares(core, buffer, products):
    def kernel(core_ref, buffer_ref, products_ref, gram_ref, theirs_ref):
        products = products_ref[...]
        start = pl.multiple_of((1 - core_ref[0]) * HALF, 128)
        theirs_ref[...] = plain_dot(buffer_ref[:, pl.ds(start, HALF)], products, (0, 0)).astype(bf16)
        gram_ref[...] = plain_dot(products, products, (0, 0))

    return pl.pallas_call(
        kernel,
        out_shape=(
            jax.ShapeDtypeStruct((RANK, RANK), f32),
            jax.ShapeDtypeStruct((HALF, RANK), bf16),
        ),
        in_specs=[SCALAR] + in_vmem(2),
        out_specs=tuple(in_vmem(2)),
        compiler_params=PARAMS,
    )(core, buffer, products)


def second_share(core, buffer, products):
    def kernel(core_ref, buffer_ref, products_ref, mine_ref):
        start = pl.multiple_of(core_ref[0] * HALF, 128)
        mine_ref[...] = plain_dot(buffer_ref[:, pl.ds(start, HALF)], products_ref[...], (0, 0))

    return pl.pallas_call(
        kernel,
        out_shape=jax.ShapeDtypeStruct((HALF, RANK), f32),
        in_specs=[SCALAR] + in_vmem(2),
        out_specs=in_vmem(1)[0],
        compiler_params=PARAMS,
    )(core, buffer, products)


def pack_shares(core, mine, theirs, gram, gram_other):
    def kernel(core_ref, mine_ref, theirs_ref, gram_ref, other_ref, out_ref):
        start = pl.multiple_of(core_ref[0] * (RANK // 2), 8)
        energy = jnp.zeros((1, RANK), f32)
        size = jnp.zeros((1, RANK), f32)
        for i in range(PEERS):
            one = mine_ref[SHARE * i : SHARE * (i + 1), :]
            two = theirs_ref[SHARE * i : SHARE * (i + 1), :].astype(f32)
            both = one + two
            energy = energy + jnp.sum(one * one + two * two, axis=0, keepdims=True)
            size = size + jnp.sum(both * both, axis=0, keepdims=True)
            rows = pl.ds(start + GRAM * i, GRAM)
            parts = split(gram_ref[rows, :] + other_ref[rows, :])
            out_ref[i] = jnp.concatenate([both, *parts], axis=0).astype(bf16)
        growth = jnp.sum(energy / size, axis=1, keepdims=True) * (1.0 / RANK)

        @pl.when(jnp.logical_not(jnp.max(growth) <= LIMIT))
        def _():
            out_ref[...] = jnp.full(out_ref.shape, jnp.nan, bf16)

    return pl.pallas_call(
        kernel,
        out_shape=jax.ShapeDtypeStruct((PEERS, PACK, RANK), bf16),
        in_specs=[SCALAR] + in_vmem(4),
        out_specs=in_vmem(1)[0],
        compiler_params=PARAMS,
    )(core, mine, theirs, gram, gram_other)


def sum_shares(parts):
    def kernel(parts_ref, out_ref):
        total = jnp.zeros((PACK, RANK), f32)
        energy = jnp.zeros((1, RANK), f32)
        for i in range(PEERS):
            part = parts_ref[i].astype(f32)
            total = total + part
            energy = energy + jnp.sum(part[:SHARE] * part[:SHARE], axis=0, keepdims=True)
        total = guarded(total, energy, SHARE)
        gram = (
            total[SHARE : SHARE + GRAM]
            + total[SHARE + GRAM : SHARE + 2 * GRAM]
            + total[SHARE + 2 * GRAM :]
        )
        packed = jnp.concatenate([total[:SHARE], *split(gram)], axis=0).astype(bf16)
        for i in range(PEERS):
            out_ref[i] = packed

    return pl.pallas_call(
        kernel,
        out_shape=jax.ShapeDtypeStruct(parts.shape, bf16),
        in_specs=in_vmem(1),
        out_specs=in_vmem(1)[0],
        compiler_params=PARAMS,
    )(parts)


def factor(core, mine, other, products):
    def gram_rows(ref):
        rows = []
        for i in range(PEERS):
            block = ref[i].astype(f32)
            rows.append(
                block[SHARE : SHARE + GRAM]
                + block[SHARE + GRAM : SHARE + 2 * GRAM]
                + block[SHARE + 2 * GRAM :]
            )
        return jnp.concatenate(rows, axis=0)

    def kernel(core_ref, mine_ref, other_ref, products_ref, left_ref, cols_ref, stats_ref, wide_ref):
        first = core_ref[0] == 0
        one, two = gram_rows(mine_ref), gram_rows(other_ref)
        gram = jnp.concatenate([jnp.where(first, one, two), jnp.where(first, two, one)], axis=0)
        inverse = triangle_inverse(gram)
        scaled = math.sqrt(D) * inverse
        high = scaled.astype(bf16)
        low = (scaled - high.astype(f32)).astype(bf16)
        products = products_ref[...]
        left_ref[...] = (
            plain_dot(products, high, (1, 1)) + plain_dot(products, low, (1, 1))
        ).astype(bf16)
        squares = jnp.zeros((1, RANK), f32)
        energy = jnp.zeros((1, RANK), f32)
        for ref, half in ((mine_ref, core_ref[0]), (other_ref, 1 - core_ref[0])):
            rows = ref[...].reshape(PEERS * PACK, RANK)
            wide_ref[...] = plain_dot(rows, high, (1, 1)) + plain_dot(rows, low, (1, 1))
            for i in range(PEERS):
                cols = wide_ref[PACK * i : PACK * i + SHARE, :]
                start = pl.multiple_of(half * HALF + SHARE * i, 8)
                cols_ref[pl.ds(start, SHARE), :] = cols
                squares = squares + jnp.sum(cols * cols, axis=0, keepdims=True)
                share = ref[i].astype(f32)[:SHARE]
                energy = energy + jnp.sum(share * share, axis=0, keepdims=True)
        eye = lax.broadcasted_iota(jnp.int32, (RANK, RANK), 0) == lax.broadcasted_iota(
            jnp.int32, (RANK, RANK), 1
        )
        diagonal = jnp.sum(jnp.where(eye, gram, 0.0), axis=0, keepdims=True)
        weights = jnp.sum(inverse * inverse, axis=0, keepdims=True)
        growth = jnp.sum(diagonal * weights, axis=1, keepdims=True) * (1.0 / RANK)
        noise = plain_dot(jnp.broadcast_to(energy, (8, RANK)), scaled * scaled, (1, 1))[:1]
        growth_cols = jnp.sum(noise / squares, axis=1, keepdims=True) * (1.0 / RANK)
        good = (growth <= LIMIT) & (growth_cols <= LIMIT)
        flag = jnp.broadcast_to(jnp.where(good, 0.0, 1.0), (1, RANK))
        zeros = jnp.zeros((6, RANK), f32)
        stats = jnp.concatenate([squares, flag, zeros], axis=0)
        for i in range(DEPTHS):
            stats_ref[i] = stats

    return pl.pallas_call(
        kernel,
        out_shape=(
            jax.ShapeDtypeStruct((ROWS, RANK), bf16),
            jax.ShapeDtypeStruct((COLS, RANK), f32),
            jax.ShapeDtypeStruct((DEPTHS, 8, RANK), f32),
        ),
        in_specs=[SCALAR] + in_vmem(3),
        out_specs=tuple(in_vmem(3)),
        scratch_shapes=[pltpu.VMEM((PEERS * PACK, RANK), f32)],
        compiler_params=PARAMS,
    )(core, mine, other, products)


def careful(weight, momentum, grad, q_factor):
    core = lax.axis_index(CORE)
    buffer = (momentum.astype(f32) + grad.astype(f32)).astype(bf16)
    partial_value = jnp.dot(buffer, q_factor, preferred_element_type=f32)
    products = gather(scatter_sum(partial_value, DEPTH, DEPTHS), DEPTH, DEPTHS)
    products = products.reshape(ROWS, RANK)
    gram = exact_dot(products, products, (0, 0))
    gram = gram + swap_core(gram)
    gram = gather(scatter_sum(gram, PLANE, PEERS), PLANE, PEERS).reshape(RANK, RANK)
    inverse = cholesky_inverse(gram)
    left_factor = (math.sqrt(D) * exact_dot(products, inverse, (1, 1))).astype(bf16)
    col_partial = plain_dot(buffer, left_factor, (0, 0))
    mine = lax.dynamic_slice_in_dim(col_partial, core * HALF, HALF, 0)
    theirs = lax.dynamic_slice_in_dim(col_partial, (1 - core) * HALF, HALF, 0)
    share = scatter_sum(mine + swap_core(theirs), PLANE, PEERS)
    squares = jnp.sum(gather(jnp.sum(share * share, axis=0)[None], EVERY, 256), axis=(0, 1))
    normalized = (share * lax.rsqrt(squares / FF + epsilon)).astype(bf16)
    mine = gather(normalized, PLANE, PEERS).reshape(HALF, RANK)
    new_factor = in_order(core, mine, swap_core(mine))
    scaled = (left_factor.astype(f32) * jnp.sqrt(squares / FF + epsilon)).astype(bf16)
    feedback = plain_dot(scaled, new_factor, (1, 1))
    new_momentum = (buffer.astype(f32) - (1.0 - keep_rate) / D * feedback).astype(bf16)
    update = plain_dot(left_factor, new_factor, (1, 1))
    new_weight = (weight.astype(f32) - step_rate / math.sqrt(RANK) * update).astype(bf16)
    return (new_weight, new_momentum, new_factor)


def on_device(weight, momentum, grad, q_factor):
    core = lax.axis_index(CORE).astype(jnp.int32).reshape(1)
    buffer = (momentum.astype(f32) + grad.astype(f32)).astype(bf16)
    partial_value = jnp.dot(buffer, q_factor, preferred_element_type=f32).astype(bf16)
    parts = exchange(partial_value.reshape(DEPTHS, ROWS // DEPTHS, RANK), DEPTH)
    products = exchange(sum_products(parts), DEPTH).reshape(ROWS, RANK)

    gram, theirs = first_shares(core, buffer, products)
    gram_other, theirs = swap_core(gram), swap_core(theirs)
    mine = second_share(core, buffer, products)
    parts = exchange(pack_shares(core, mine, theirs, gram, gram_other), PLANE)
    mine = exchange(sum_shares(parts), PLANE)
    other = swap_core(mine)
    left, cols, stats = factor(core, mine, other, products)
    stats = exchange(stats, DEPTH)
    feedback = plain_dot(left, cols.astype(bf16), (1, 1))
    new_momentum = (buffer.astype(f32) - (1.0 - keep_rate) / D * feedback).astype(bf16)
    squares = jnp.sum(stats[:, 0, :], axis=0)
    new_factor = (cols * lax.rsqrt(squares / FF + epsilon)).astype(bf16)
    update = plain_dot(left, new_factor, (1, 1))
    new_weight = (weight.astype(f32) - step_rate / math.sqrt(RANK) * update).astype(bf16)

    def again(state):
        return (jnp.zeros((), f32), *careful(weight, momentum, grad, q_factor))

    flags = jnp.sum(stats[:, 1, 0])
    state = lax.while_loop(
        lambda state: state[0] > 0.5, again, (flags, new_weight, new_momentum, new_factor)
    )
    return state[1:]


def solution(mesh):
    fine = Mesh(mesh.devices.reshape(4, 4, 2, 8), EVERY)
    rows = ("x", "y", CORE)
    placed = (P(rows, DEPTH), P(rows, DEPTH), P(rows, DEPTH), P(DEPTH, None))
    return jax.shard_map(
        on_device,
        mesh=fine,
        in_specs=placed,
        out_specs=(P(rows, DEPTH), P(rows, DEPTH), P(DEPTH, None)),
        check_vma=False,
    )
```

```python
import math

import jax
import jax.numpy as jnp
from jax import lax
from jax.experimental import pallas as pl
from jax.experimental.pallas import tpu as pltpu
from jax.sharding import Mesh, PartitionSpec as P

D = 8192
FF = 26624
RANK = 256

epsilon = 1e-06
keep_rate = 0.9
step_rate = 0.5

HIGHEST = lax.Precision.HIGHEST
f32 = jnp.float32
bf16 = jnp.bfloat16

CORE = "core"
PLANE = ("x", "y")
DEPTH = "z"
EVERY = ("x", "y", "core", "z")

ROWS = 256
COLS = 3328
HALF = 1664
PEERS = 16
SHARE = 104
GRAM = 8
PACK = 128
DEPTHS = 8
LIMIT = 4.0


def exact_dot(a, b, contract):
    dims = (((contract[0],), (contract[1],)), ((), ()))
    return lax.dot_general(a, b, dims, precision=HIGHEST, preferred_element_type=f32)


def plain_dot(a, b, contract):
    dims = (((contract[0],), (contract[1],)), ((), ()))
    return lax.dot_general(a, b, dims, preferred_element_type=f32)


def in_vmem(count):
    return [pl.BlockSpec(memory_space=pltpu.VMEM)] * count


SCALAR = pl.BlockSpec(memory_space=pltpu.SMEM)
PARAMS = pltpu.CompilerParams(vmem_limit_bytes=20 * 2**20)


LEAF = 64
PANEL = 16


def leaf_inverse(a):
    n = a.shape[0]
    lanes = 2 * n
    rows = lax.broadcasted_iota(jnp.int32, (n, n), 0)
    cols = lax.broadcasted_iota(jnp.int32, (n, n), 1)
    eye = (rows == cols).astype(f32)
    both = jnp.concatenate([a, eye], axis=1)
    count = n // 8
    slabs = [both[8 * i : 8 * i + 8, :] for i in range(count)]
    row8 = lax.broadcasted_iota(jnp.int32, (8, lanes), 0)
    for first in range(0, count, PANEL // 8):
        panel = [
            [
                jnp.broadcast_to(slabs[i][:, 8 * first + k : 8 * first + k + 1], (8, lanes))
                for i in range(first, count)
            ]
            for k in range(PANEL)
        ]
        for k in range(PANEL):
            at, sub = first + k // 8, k % 8
            pivot = jnp.broadcast_to(panel[k][at - first][sub : sub + 1, :], (8, lanes))
            inverse = 1.0 / pivot
            factor = {}
            for i in range(at, count):
                value = panel[k][i - first] * inverse
                factor[i] = jnp.where(row8 > sub, value, 0.0) if i == at else value
            for m in range(k + 1, PANEL):
                row = jnp.broadcast_to(panel[m][at - first][sub : sub + 1, :], (8, lanes))
                for i in range(at, count):
                    panel[m][i - first] = panel[m][i - first] - factor[i] * row
            row = jnp.broadcast_to(slabs[at][sub : sub + 1, :], (8, lanes))
            for i in range(at, count):
                slabs[i] = slabs[i] - factor[i] * row
    both = jnp.concatenate(slabs, axis=0)
    pivots = jnp.sum(both[:, :n] * eye, axis=1, keepdims=True)
    return both[:, n:] * lax.rsqrt(pivots)


def triangle_inverse(a):
    n = a.shape[0]
    if n <= LEAF:
        return leaf_inverse(a)
    h = n // 2
    upper = triangle_inverse(a[:h, :h])
    below = exact_dot(a[h:, :h], upper, (1, 1))
    rest = a[h:, h:] - exact_dot(below, below, (1, 1))
    mixed = exact_dot(below, upper, (1, 0))
    lower = triangle_inverse(rest)
    corner = -exact_dot(lower, mixed, (1, 0))
    top = jnp.concatenate([upper, jnp.zeros((h, n - h), f32)], axis=1)
    return jnp.concatenate([top, jnp.concatenate([corner, lower], axis=1)], axis=0)


def cholesky_inverse(gram):
    def kernel(gram_ref, inverse_ref):
        inverse_ref[...] = triangle_inverse(gram_ref[...])

    return pl.pallas_call(
        kernel,
        out_shape=jax.ShapeDtypeStruct((RANK, RANK), f32),
        in_specs=in_vmem(1),
        out_specs=in_vmem(1)[0],
        compiler_params=PARAMS,
    )(gram)


def exchange(pieces, axis):
    return lax.all_to_all(pieces, axis, 0, 0)


def scatter_sum(value, axis, parts):
    pieces = value.reshape(parts, value.shape[0] // parts, *value.shape[1:])
    return jnp.sum(exchange(pieces, axis).astype(f32), axis=0)


def gather(value, axis, parts):
    return exchange(jnp.broadcast_to(value[None], (parts, *value.shape)), axis)


def swap_core(value):
    return lax.ppermute(value, CORE, [(0, 1), (1, 0)])


def in_order(core, mine, other):
    first = core == 0
    return jnp.concatenate([jnp.where(first, mine, other), jnp.where(first, other, mine)], axis=0)


def guarded(total, energy, rows):
    size = jnp.sum(total[:rows] * total[:rows], axis=0, keepdims=True)
    growth = jnp.sum(energy / size, axis=1, keepdims=True) * (1.0 / RANK)
    return jnp.where(growth <= LIMIT, total, jnp.nan)


def split(value):
    high = value.astype(bf16).astype(f32)
    rest = value - high
    middle = rest.astype(bf16).astype(f32)
    return high, middle, rest - middle


CUTS = (0, 896, 1792, 2560, 3328)


def buffer_and_products(momentum, grad, q_factor):
    def kernel(
        momentum_hbm, grad_hbm, q_hbm, buffer_ref, out_ref, momentum_ref, grad_ref, q_ref, sems
    ):
        copies = []
        for i, (low, high) in enumerate(zip(CUTS[:-1], CUTS[1:])):
            cut = pl.ds(low, high - low)
            three = (
                pltpu.make_async_copy(momentum_hbm.at[:, cut], momentum_ref.at[:, cut], sems.at[i, 0]),
                pltpu.make_async_copy(grad_hbm.at[:, cut], grad_ref.at[:, cut], sems.at[i, 1]),
                pltpu.make_async_copy(q_hbm.at[cut, :], q_ref.at[cut, :], sems.at[i, 2]),
            )
            for copy in three:
                copy.start()
            copies.append(three)
        total = jnp.zeros((ROWS, RANK), f32)
        for (low, high), three in zip(zip(CUTS[:-1], CUTS[1:]), copies):
            for copy in three:
                copy.wait()
            part = (
                momentum_ref[:, low:high].astype(f32) + grad_ref[:, low:high].astype(f32)
            ).astype(bf16)
            buffer_ref[:, low:high] = part
            total = total + plain_dot(part, q_ref[low:high, :], (1, 0))
        out_ref[...] = total.astype(bf16)

    return pl.pallas_call(
        kernel,
        out_shape=(
            jax.ShapeDtypeStruct((ROWS, COLS), bf16),
            jax.ShapeDtypeStruct((ROWS, RANK), bf16),
        ),
        in_specs=[pl.BlockSpec(memory_space=pltpu.HBM)] * 3,
        out_specs=tuple(in_vmem(2)),
        scratch_shapes=[
            pltpu.VMEM((ROWS, COLS), bf16),
            pltpu.VMEM((ROWS, COLS), bf16),
            pltpu.VMEM((COLS, RANK), bf16),
            pltpu.SemaphoreType.DMA((len(CUTS) - 1, 3)),
        ],
        compiler_params=PARAMS,
    )(momentum, grad, q_factor)


def sum_products(parts):
    def kernel(parts_ref, out_ref):
        total = jnp.zeros((ROWS // DEPTHS, RANK), f32)
        energy = jnp.zeros((1, RANK), f32)
        for i in range(DEPTHS):
            part = parts_ref[i].astype(f32)
            total = total + part
            energy = energy + jnp.sum(part * part, axis=0, keepdims=True)
        total = guarded(total, energy, ROWS // DEPTHS).astype(bf16)
        for i in range(DEPTHS):
            out_ref[i] = total

    return pl.pallas_call(
        kernel,
        out_shape=jax.ShapeDtypeStruct(parts.shape, bf16),
        in_specs=in_vmem(1),
        out_specs=in_vmem(1)[0],
        compiler_params=PARAMS,
    )(parts)


def first_shares(core, buffer, products):
    def kernel(core_ref, buffer_ref, products_ref, gram_ref, theirs_ref):
        products = products_ref[...]
        start = pl.multiple_of((1 - core_ref[0]) * HALF, 128)
        theirs_ref[...] = plain_dot(buffer_ref[:, pl.ds(start, HALF)], products, (0, 0)).astype(bf16)
        gram_ref[...] = plain_dot(products, products, (0, 0))

    return pl.pallas_call(
        kernel,
        out_shape=(
            jax.ShapeDtypeStruct((RANK, RANK), f32),
            jax.ShapeDtypeStruct((HALF, RANK), bf16),
        ),
        in_specs=[SCALAR] + in_vmem(2),
        out_specs=tuple(in_vmem(2)),
        compiler_params=PARAMS,
    )(core, buffer, products)


def second_share(core, buffer, products):
    def kernel(core_ref, buffer_ref, products_ref, mine_ref):
        start = pl.multiple_of(core_ref[0] * HALF, 128)
        mine_ref[...] = plain_dot(buffer_ref[:, pl.ds(start, HALF)], products_ref[...], (0, 0))

    return pl.pallas_call(
        kernel,
        out_shape=jax.ShapeDtypeStruct((HALF, RANK), f32),
        in_specs=[SCALAR] + in_vmem(2),
        out_specs=in_vmem(1)[0],
        compiler_params=PARAMS,
    )(core, buffer, products)


def pack_shares(core, mine, theirs, gram, gram_other):
    def kernel(core_ref, mine_ref, theirs_ref, gram_ref, other_ref, out_ref):
        start = pl.multiple_of(core_ref[0] * (RANK // 2), 8)
        energy = jnp.zeros((1, RANK), f32)
        size = jnp.zeros((1, RANK), f32)
        for i in range(PEERS):
            one = mine_ref[SHARE * i : SHARE * (i + 1), :]
            two = theirs_ref[SHARE * i : SHARE * (i + 1), :].astype(f32)
            both = one + two
            energy = energy + jnp.sum(one * one + two * two, axis=0, keepdims=True)
            size = size + jnp.sum(both * both, axis=0, keepdims=True)
            rows = pl.ds(start + GRAM * i, GRAM)
            parts = split(gram_ref[rows, :] + other_ref[rows, :])
            out_ref[i] = jnp.concatenate([both, *parts], axis=0).astype(bf16)
        growth = jnp.sum(energy / size, axis=1, keepdims=True) * (1.0 / RANK)

        @pl.when(jnp.logical_not(jnp.max(growth) <= LIMIT))
        def _():
            out_ref[...] = jnp.full(out_ref.shape, jnp.nan, bf16)

    return pl.pallas_call(
        kernel,
        out_shape=jax.ShapeDtypeStruct((PEERS, PACK, RANK), bf16),
        in_specs=[SCALAR] + in_vmem(4),
        out_specs=in_vmem(1)[0],
        compiler_params=PARAMS,
    )(core, mine, theirs, gram, gram_other)


def sum_shares(parts):
    def kernel(parts_ref, out_ref):
        total = jnp.zeros((PACK, RANK), f32)
        energy = jnp.zeros((1, RANK), f32)
        for i in range(PEERS):
            part = parts_ref[i].astype(f32)
            total = total + part
            energy = energy + jnp.sum(part[:SHARE] * part[:SHARE], axis=0, keepdims=True)
        total = guarded(total, energy, SHARE)
        gram = (
            total[SHARE : SHARE + GRAM]
            + total[SHARE + GRAM : SHARE + 2 * GRAM]
            + total[SHARE + 2 * GRAM :]
        )
        packed = jnp.concatenate([total[:SHARE], *split(gram)], axis=0).astype(bf16)
        for i in range(PEERS):
            out_ref[i] = packed

    return pl.pallas_call(
        kernel,
        out_shape=jax.ShapeDtypeStruct(parts.shape, bf16),
        in_specs=in_vmem(1),
        out_specs=in_vmem(1)[0],
        compiler_params=PARAMS,
    )(parts)


def factor(core, mine, other, products):
    def gram_rows(ref):
        rows = []
        for i in range(PEERS):
            block = ref[i].astype(f32)
            rows.append(
                block[SHARE : SHARE + GRAM]
                + block[SHARE + GRAM : SHARE + 2 * GRAM]
                + block[SHARE + 2 * GRAM :]
            )
        return jnp.concatenate(rows, axis=0)

    def kernel(
        core_ref, mine_ref, other_ref, products_ref, left_ref, cols_ref, stats_ref, wide_ref, full_ref
    ):
        first = core_ref[0] == 0
        one, two = gram_rows(mine_ref), gram_rows(other_ref)
        gram = jnp.concatenate([jnp.where(first, one, two), jnp.where(first, two, one)], axis=0)
        inverse = triangle_inverse(gram)
        scaled = math.sqrt(D) * inverse
        high = scaled.astype(bf16)
        low = (scaled - high.astype(f32)).astype(bf16)
        products = products_ref[...]
        left_ref[...] = (
            plain_dot(products, high, (1, 1)) + plain_dot(products, low, (1, 1))
        ).astype(bf16)
        squares = jnp.zeros((1, RANK), f32)
        energy = jnp.zeros((1, RANK), f32)
        for ref, half in ((mine_ref, core_ref[0]), (other_ref, 1 - core_ref[0])):
            rows = ref[...].reshape(PEERS * PACK, RANK)
            wide_ref[...] = plain_dot(rows, high, (1, 1)) + plain_dot(rows, low, (1, 1))
            for i in range(PEERS):
                cols = wide_ref[PACK * i : PACK * i + SHARE, :]
                start = pl.multiple_of(half * HALF + SHARE * i, 8)
                full_ref[pl.ds(start, SHARE), :] = cols
                squares = squares + jnp.sum(cols * cols, axis=0, keepdims=True)
                share = ref[i].astype(f32)[:SHARE]
                energy = energy + jnp.sum(share * share, axis=0, keepdims=True)
        cols_ref[...] = full_ref[...].astype(bf16)
        eye = lax.broadcasted_iota(jnp.int32, (RANK, RANK), 0) == lax.broadcasted_iota(
            jnp.int32, (RANK, RANK), 1
        )
        diagonal = jnp.sum(jnp.where(eye, gram, 0.0), axis=0, keepdims=True)
        weights = jnp.sum(inverse * inverse, axis=0, keepdims=True)
        growth = jnp.sum(diagonal * weights, axis=1, keepdims=True) * (1.0 / RANK)
        noise = plain_dot(jnp.broadcast_to(energy, (8, RANK)), scaled * scaled, (1, 1))[:1]
        growth_cols = jnp.sum(noise / squares, axis=1, keepdims=True) * (1.0 / RANK)
        good = (growth <= LIMIT) & (growth_cols <= LIMIT)
        flag = jnp.broadcast_to(jnp.where(good, 0.0, 1.0), (1, RANK))
        zeros = jnp.zeros((6, RANK), f32)
        stats = jnp.concatenate([squares, flag, zeros], axis=0)
        for i in range(DEPTHS):
            stats_ref[i] = stats

    return pl.pallas_call(
        kernel,
        out_shape=(
            jax.ShapeDtypeStruct((ROWS, RANK), bf16),
            jax.ShapeDtypeStruct((COLS, RANK), bf16),
            jax.ShapeDtypeStruct((DEPTHS, 8, RANK), f32),
        ),
        in_specs=[SCALAR] + in_vmem(3),
        out_specs=tuple(in_vmem(3)),
        scratch_shapes=[pltpu.VMEM((PEERS * PACK, RANK), f32), pltpu.VMEM((COLS, RANK), f32)],
        compiler_params=PARAMS,
    )(core, mine, other, products)


def careful(weight, momentum, grad, q_factor):
    core = lax.axis_index(CORE)
    buffer = (momentum.astype(f32) + grad.astype(f32)).astype(bf16)
    partial_value = jnp.dot(buffer, q_factor, preferred_element_type=f32)
    products = gather(scatter_sum(partial_value, DEPTH, DEPTHS), DEPTH, DEPTHS)
    products = products.reshape(ROWS, RANK)
    gram = exact_dot(products, products, (0, 0))
    gram = gram + swap_core(gram)
    gram = gather(scatter_sum(gram, PLANE, PEERS), PLANE, PEERS).reshape(RANK, RANK)
    inverse = cholesky_inverse(gram)
    left_factor = (math.sqrt(D) * exact_dot(products, inverse, (1, 1))).astype(bf16)
    col_partial = plain_dot(buffer, left_factor, (0, 0))
    mine = lax.dynamic_slice_in_dim(col_partial, core * HALF, HALF, 0)
    theirs = lax.dynamic_slice_in_dim(col_partial, (1 - core) * HALF, HALF, 0)
    share = scatter_sum(mine + swap_core(theirs), PLANE, PEERS)
    squares = jnp.sum(gather(jnp.sum(share * share, axis=0)[None], EVERY, 256), axis=(0, 1))
    normalized = (share * lax.rsqrt(squares / FF + epsilon)).astype(bf16)
    mine = gather(normalized, PLANE, PEERS).reshape(HALF, RANK)
    new_factor = in_order(core, mine, swap_core(mine))
    scaled = (left_factor.astype(f32) * jnp.sqrt(squares / FF + epsilon)).astype(bf16)
    feedback = plain_dot(scaled, new_factor, (1, 1))
    new_momentum = (buffer.astype(f32) - (1.0 - keep_rate) / D * feedback).astype(bf16)
    update = plain_dot(left_factor, new_factor, (1, 1))
    new_weight = (weight.astype(f32) - step_rate / math.sqrt(RANK) * update).astype(bf16)
    return (new_weight, new_momentum, new_factor)


def on_device(weight, momentum, grad, q_factor):
    core = lax.axis_index(CORE).astype(jnp.int32).reshape(1)
    buffer, partial_value = buffer_and_products(momentum, grad, q_factor)
    parts = exchange(partial_value.reshape(DEPTHS, ROWS // DEPTHS, RANK), DEPTH)
    products = exchange(sum_products(parts), DEPTH).reshape(ROWS, RANK)

    gram, theirs = first_shares(core, buffer, products)
    gram_other, theirs = swap_core(gram), swap_core(theirs)
    mine = second_share(core, buffer, products)
    parts = exchange(pack_shares(core, mine, theirs, gram, gram_other), PLANE)
    mine = exchange(sum_shares(parts), PLANE)
    other = swap_core(mine)
    left, cols, stats = factor(core, mine, other, products)
    stats = exchange(stats, DEPTH)
    feedback = plain_dot(left, cols, (1, 1))
    new_momentum = (buffer.astype(f32) - (1.0 - keep_rate) / D * feedback).astype(bf16)
    squares = jnp.sum(stats[:, 0, :], axis=0)
    new_factor = (cols.astype(f32) * lax.rsqrt(squares / FF + epsilon)).astype(bf16)
    update = plain_dot(left, new_factor, (1, 1))
    new_weight = (weight.astype(f32) - step_rate / math.sqrt(RANK) * update).astype(bf16)

    def again(state):
        return (jnp.zeros((), f32), *careful(weight, momentum, grad, q_factor))

    flags = jnp.sum(stats[:, 1, 0])
    state = lax.while_loop(
        lambda state: state[0] > 0.5, again, (flags, new_weight, new_momentum, new_factor)
    )
    return state[1:]


def solution(mesh):
    fine = Mesh(mesh.devices.reshape(4, 4, 2, 8), EVERY)
    rows = ("x", "y", CORE)
    placed = (P(rows, DEPTH), P(rows, DEPTH), P(rows, DEPTH), P(DEPTH, None))
    return jax.shard_map(
        on_device,
        mesh=fine,
        in_specs=placed,
        out_specs=(P(rows, DEPTH), P(rows, DEPTH), P(DEPTH, None)),
        check_vma=False,
    )
```

```python
import math

import jax
import jax.numpy as jnp
from jax import lax
from jax.experimental import pallas as pl
from jax.experimental.pallas import tpu as pltpu
from jax.sharding import Mesh, PartitionSpec as P

D = 8192
FF = 26624
RANK = 256

epsilon = 1e-06
keep_rate = 0.9
step_rate = 0.5

HIGHEST = lax.Precision.HIGHEST
f32 = jnp.float32
bf16 = jnp.bfloat16

CORE = "core"
PLANE = ("x", "y")
DEPTH = "z"
EVERY = ("x", "y", "core", "z")

ROWS = 256
COLS = 3328
HALF = 1664
PEERS = 16
SHARE = 104
GRAM = 8
QUARTER = 128
PACK = 128
DEPTHS = 8
LIMIT = 4.0


def exact_dot(a, b, contract):
    dims = (((contract[0],), (contract[1],)), ((), ()))
    return lax.dot_general(a, b, dims, precision=HIGHEST, preferred_element_type=f32)


def plain_dot(a, b, contract):
    dims = (((contract[0],), (contract[1],)), ((), ()))
    return lax.dot_general(a, b, dims, preferred_element_type=f32)


def in_vmem(count):
    return [pl.BlockSpec(memory_space=pltpu.VMEM)] * count


SCALAR = pl.BlockSpec(memory_space=pltpu.SMEM)
PARAMS = pltpu.CompilerParams(vmem_limit_bytes=20 * 2**20)


LEAF = 64
PANEL = 16


def leaf_inverse(a):
    n = a.shape[0]
    lanes = 2 * n
    rows = lax.broadcasted_iota(jnp.int32, (n, n), 0)
    cols = lax.broadcasted_iota(jnp.int32, (n, n), 1)
    eye = (rows == cols).astype(f32)
    both = jnp.concatenate([a, eye], axis=1)
    count = n // 8
    slabs = [both[8 * i : 8 * i + 8, :] for i in range(count)]
    row8 = lax.broadcasted_iota(jnp.int32, (8, lanes), 0)
    for first in range(0, count, PANEL // 8):
        panel = [
            [
                jnp.broadcast_to(slabs[i][:, 8 * first + k : 8 * first + k + 1], (8, lanes))
                for i in range(first, count)
            ]
            for k in range(PANEL)
        ]
        for k in range(PANEL):
            at, sub = first + k // 8, k % 8
            pivot = jnp.broadcast_to(panel[k][at - first][sub : sub + 1, :], (8, lanes))
            inverse = 1.0 / pivot
            factor = {}
            for i in range(at, count):
                value = panel[k][i - first] * inverse
                factor[i] = jnp.where(row8 > sub, value, 0.0) if i == at else value
            for m in range(k + 1, PANEL):
                row = jnp.broadcast_to(panel[m][at - first][sub : sub + 1, :], (8, lanes))
                for i in range(at, count):
                    panel[m][i - first] = panel[m][i - first] - factor[i] * row
            row = jnp.broadcast_to(slabs[at][sub : sub + 1, :], (8, lanes))
            for i in range(at, count):
                slabs[i] = slabs[i] - factor[i] * row
    both = jnp.concatenate(slabs, axis=0)
    pivots = jnp.sum(both[:, :n] * eye, axis=1, keepdims=True)
    return both[:, n:] * lax.rsqrt(pivots)


def triangle_inverse(a):
    n = a.shape[0]
    if n <= LEAF:
        return leaf_inverse(a)
    h = n // 2
    upper = triangle_inverse(a[:h, :h])
    below = exact_dot(a[h:, :h], upper, (1, 1))
    rest = a[h:, h:] - exact_dot(below, below, (1, 1))
    mixed = exact_dot(below, upper, (1, 0))
    lower = triangle_inverse(rest)
    corner = -exact_dot(lower, mixed, (1, 0))
    top = jnp.concatenate([upper, jnp.zeros((h, n - h), f32)], axis=1)
    return jnp.concatenate([top, jnp.concatenate([corner, lower], axis=1)], axis=0)


def cholesky_inverse(gram):
    def kernel(gram_ref, inverse_ref):
        inverse_ref[...] = triangle_inverse(gram_ref[...])

    return pl.pallas_call(
        kernel,
        out_shape=jax.ShapeDtypeStruct((RANK, RANK), f32),
        in_specs=in_vmem(1),
        out_specs=in_vmem(1)[0],
        compiler_params=PARAMS,
    )(gram)


def exchange(pieces, axis):
    return lax.all_to_all(pieces, axis, 0, 0)


def scatter_sum(value, axis, parts):
    pieces = value.reshape(parts, value.shape[0] // parts, *value.shape[1:])
    return jnp.sum(exchange(pieces, axis).astype(f32), axis=0)


def gather(value, axis, parts):
    return exchange(jnp.broadcast_to(value[None], (parts, *value.shape)), axis)


def swap_core(value):
    return lax.ppermute(value, CORE, [(0, 1), (1, 0)])


def in_order(core, mine, other):
    first = core == 0
    return jnp.concatenate([jnp.where(first, mine, other), jnp.where(first, other, mine)], axis=0)


def guarded(total, energy, rows):
    size = jnp.sum(total[:rows] * total[:rows], axis=0, keepdims=True)
    growth = jnp.sum(energy / size, axis=1, keepdims=True) * (1.0 / RANK)
    return jnp.where(growth <= LIMIT, total, jnp.nan)


def split(value):
    high = value.astype(bf16).astype(f32)
    rest = value - high
    middle = rest.astype(bf16).astype(f32)
    return high, middle, rest - middle


CUTS = (0, 896, 1792, 2560, 3328)


def buffer_and_products(momentum, grad, q_factor):
    def kernel(
        momentum_hbm, grad_hbm, q_hbm, buffer_ref, out_ref, momentum_ref, grad_ref, q_ref, sems
    ):
        copies = []
        for i, (low, high) in enumerate(zip(CUTS[:-1], CUTS[1:])):
            cut = pl.ds(low, high - low)
            three = (
                pltpu.make_async_copy(momentum_hbm.at[:, cut], momentum_ref.at[:, cut], sems.at[i, 0]),
                pltpu.make_async_copy(grad_hbm.at[:, cut], grad_ref.at[:, cut], sems.at[i, 1]),
                pltpu.make_async_copy(q_hbm.at[cut, :], q_ref.at[cut, :], sems.at[i, 2]),
            )
            for copy in three:
                copy.start()
            copies.append(three)
        total = jnp.zeros((ROWS, RANK), f32)
        for (low, high), three in zip(zip(CUTS[:-1], CUTS[1:]), copies):
            for copy in three:
                copy.wait()
            part = (
                momentum_ref[:, low:high].astype(f32) + grad_ref[:, low:high].astype(f32)
            ).astype(bf16)
            buffer_ref[:, low:high] = part
            total = total + plain_dot(part, q_ref[low:high, :], (1, 0))
        out_ref[...] = total.astype(bf16)

    return pl.pallas_call(
        kernel,
        out_shape=(
            jax.ShapeDtypeStruct((ROWS, COLS), bf16),
            jax.ShapeDtypeStruct((ROWS, RANK), bf16),
        ),
        in_specs=[pl.BlockSpec(memory_space=pltpu.HBM)] * 3,
        out_specs=tuple(in_vmem(2)),
        scratch_shapes=[
            pltpu.VMEM((ROWS, COLS), bf16),
            pltpu.VMEM((ROWS, COLS), bf16),
            pltpu.VMEM((COLS, RANK), bf16),
            pltpu.SemaphoreType.DMA((len(CUTS) - 1, 3)),
        ],
        compiler_params=PARAMS,
    )(momentum, grad, q_factor)


def sum_products(parts):
    def kernel(parts_ref, out_ref):
        total = jnp.zeros((ROWS // DEPTHS, RANK), f32)
        energy = jnp.zeros((1, RANK), f32)
        for i in range(DEPTHS):
            part = parts_ref[i].astype(f32)
            total = total + part
            energy = energy + jnp.sum(part * part, axis=0, keepdims=True)
        total = guarded(total, energy, ROWS // DEPTHS).astype(bf16)
        for i in range(DEPTHS):
            out_ref[i] = total

    return pl.pallas_call(
        kernel,
        out_shape=jax.ShapeDtypeStruct(parts.shape, bf16),
        in_specs=in_vmem(1),
        out_specs=in_vmem(1)[0],
        compiler_params=PARAMS,
    )(parts)


def first_shares(core, buffer, products):
    def kernel(core_ref, buffer_ref, products_ref, gram_ref, theirs_ref):
        products = products_ref[...]
        start = pl.multiple_of((1 - core_ref[0]) * HALF, 128)
        theirs_ref[...] = plain_dot(buffer_ref[:, pl.ds(start, HALF)], products, (0, 0)).astype(bf16)
        gram_ref[...] = plain_dot(products, products, (0, 0))

    return pl.pallas_call(
        kernel,
        out_shape=(
            jax.ShapeDtypeStruct((RANK, RANK), f32),
            jax.ShapeDtypeStruct((HALF, RANK), bf16),
        ),
        in_specs=[SCALAR] + in_vmem(2),
        out_specs=tuple(in_vmem(2)),
        compiler_params=PARAMS,
    )(core, buffer, products)


def second_share(core, buffer, products):
    def kernel(core_ref, buffer_ref, products_ref, mine_ref):
        start = pl.multiple_of(core_ref[0] * HALF, 128)
        mine_ref[...] = plain_dot(buffer_ref[:, pl.ds(start, HALF)], products_ref[...], (0, 0))

    return pl.pallas_call(
        kernel,
        out_shape=jax.ShapeDtypeStruct((HALF, RANK), f32),
        in_specs=[SCALAR] + in_vmem(2),
        out_specs=in_vmem(1)[0],
        compiler_params=PARAMS,
    )(core, buffer, products)


def pack_shares(core, mine, theirs, gram, gram_other):
    def kernel(core_ref, mine_ref, theirs_ref, gram_ref, other_ref, out_ref):
        start = pl.multiple_of(core_ref[0] * (QUARTER // 2) + QUARTER, 8)
        energy = jnp.zeros((1, RANK), f32)
        size = jnp.zeros((1, RANK), f32)
        for i in range(PEERS):
            one = mine_ref[SHARE * i : SHARE * (i + 1), :]
            two = theirs_ref[SHARE * i : SHARE * (i + 1), :].astype(f32)
            both = one + two
            energy = energy + jnp.sum(one * one + two * two, axis=0, keepdims=True)
            size = size + jnp.sum(both * both, axis=0, keepdims=True)
            upper = slice(GRAM * i, GRAM * (i + 1))
            upper = gram_ref[upper, :QUARTER] + other_ref[upper, :QUARTER]
            lower = pl.ds(start + GRAM * (i // 2), GRAM)
            lower = gram_ref[lower, :] + other_ref[lower, :]
            lower = lower[4 * (i % 2) : 4 * (i % 2) + 4, :]
            lower = jnp.concatenate([lower[:, :QUARTER], lower[:, QUARTER:]], axis=0)
            parts = split(jnp.concatenate([upper, lower], axis=1))
            out_ref[i] = jnp.concatenate([both, *parts], axis=0).astype(bf16)
        growth = jnp.sum(energy / size, axis=1, keepdims=True) * (1.0 / RANK)

        @pl.when(jnp.logical_not(jnp.max(growth) <= LIMIT))
        def _():
            out_ref[...] = jnp.full(out_ref.shape, jnp.nan, bf16)

    return pl.pallas_call(
        kernel,
        out_shape=jax.ShapeDtypeStruct((PEERS, PACK, RANK), bf16),
        in_specs=[SCALAR] + in_vmem(4),
        out_specs=in_vmem(1)[0],
        compiler_params=PARAMS,
    )(core, mine, theirs, gram, gram_other)


def sum_shares(parts):
    def kernel(parts_ref, out_ref):
        total = jnp.zeros((PACK, RANK), f32)
        energy = jnp.zeros((1, RANK), f32)
        for i in range(PEERS):
            part = parts_ref[i].astype(f32)
            total = total + part
            energy = energy + jnp.sum(part[:SHARE] * part[:SHARE], axis=0, keepdims=True)
        total = guarded(total, energy, SHARE)
        gram = (
            total[SHARE : SHARE + GRAM]
            + total[SHARE + GRAM : SHARE + 2 * GRAM]
            + total[SHARE + 2 * GRAM :]
        )
        packed = jnp.concatenate([total[:SHARE], *split(gram)], axis=0).astype(bf16)
        for i in range(PEERS):
            out_ref[i] = packed

    return pl.pallas_call(
        kernel,
        out_shape=jax.ShapeDtypeStruct(parts.shape, bf16),
        in_specs=in_vmem(1),
        out_specs=in_vmem(1)[0],
        compiler_params=PARAMS,
    )(parts)


def gram_block(ref, i):
    block = ref[i].astype(f32)
    return (
        block[SHARE : SHARE + GRAM]
        + block[SHARE + GRAM : SHARE + 2 * GRAM]
        + block[SHARE + 2 * GRAM :]
    )


def second_moment(ref):
    rows = ref[...].reshape(PEERS * PACK, RANK)
    index = lax.broadcasted_iota(jnp.int32, rows.shape, 0)
    rows = jnp.where(lax.rem(index, PACK) < SHARE, rows.astype(f32), 0.0).astype(bf16)
    return plain_dot(rows, rows, (0, 0))


def diagonal(value):
    n = value.shape[0]
    rows = lax.broadcasted_iota(jnp.int32, (n, n), 0)
    cols = lax.broadcasted_iota(jnp.int32, (n, n), 1)
    return jnp.sum(jnp.where(rows == cols, value, 0.0), axis=0, keepdims=True)


def first_factor(mine):
    def kernel(mine_ref, upper_ref, diagonal_ref, moment_ref):
        gram = jnp.concatenate(
            [gram_block(mine_ref, i)[:, :QUARTER] for i in range(PEERS)], axis=0
        )
        upper_ref[...] = triangle_inverse(gram)
        diagonal_ref[...] = jnp.broadcast_to(diagonal(gram), (8, QUARTER))
        moment_ref[...] = second_moment(mine_ref)

    return pl.pallas_call(
        kernel,
        out_shape=(
            jax.ShapeDtypeStruct((QUARTER, QUARTER), f32),
            jax.ShapeDtypeStruct((8, QUARTER), f32),
            jax.ShapeDtypeStruct((RANK, RANK), f32),
        ),
        in_specs=in_vmem(1),
        out_specs=tuple(in_vmem(3)),
        compiler_params=PARAMS,
        cost_estimate=pl.CostEstimate(flops=10**10, bytes_accessed=10**6, transcendentals=0),
    )(mine)


def second_factor(core, mine, other, upper, diagonal_upper, moment):
    def kernel(
        core_ref, mine_ref, other_ref, upper_ref, diagonal_ref, moment_ref, high_ref, low_ref,
        stats_ref, rows_ref,
    ):
        for at, ref in enumerate((mine_ref, other_ref)):
            for i in range(PEERS):
                block = gram_block(ref, i)
                rows_ref[at, 4 * i : 4 * i + 4, :QUARTER] = block[:4, QUARTER:]
                rows_ref[at, 4 * i : 4 * i + 4, QUARTER:] = block[4:, QUARTER:]
        first = core_ref[0] == 0
        one, two = rows_ref[0], rows_ref[1]
        gram = jnp.concatenate([jnp.where(first, one, two), jnp.where(first, two, one)], axis=0)
        upper = upper_ref[...]
        below = exact_dot(gram[:, :QUARTER], upper, (1, 1))
        rest = gram[:, QUARTER:]
        mixed = exact_dot(below, upper, (1, 0))
        lower = triangle_inverse(rest - exact_dot(below, below, (1, 1)))
        corner = -exact_dot(lower, mixed, (1, 0))
        zeros = jnp.zeros((QUARTER, QUARTER), f32)
        inverse = jnp.concatenate(
            [
                jnp.concatenate([upper, zeros], axis=1),
                jnp.concatenate([corner, lower], axis=1),
            ],
            axis=0,
        )
        scaled = math.sqrt(D) * inverse
        high = scaled.astype(bf16)
        high_ref[...] = high
        low_ref[...] = (scaled - high.astype(f32)).astype(bf16)
        moment = moment_ref[...] + second_moment(other_ref)
        ones = jnp.ones((8, RANK), f32)
        squares = exact_dot(ones, exact_dot(scaled, moment, (1, 0)) * scaled, (1, 1))[:1]
        gram_diagonal = jnp.concatenate([diagonal_ref[0:1, :], diagonal(rest)], axis=1)
        weights = jnp.sum(inverse * inverse, axis=0, keepdims=True)
        growth = jnp.sum(gram_diagonal * weights, axis=1, keepdims=True) * (1.0 / RANK)
        energy = jnp.broadcast_to(diagonal(moment), (8, RANK))
        noise = exact_dot(energy, scaled * scaled, (1, 1))[:1]
        ratio = jnp.where(squares > 0.0, noise / squares, jnp.inf)
        growth_cols = jnp.sum(ratio, axis=1, keepdims=True) * (1.0 / RANK)
        good = (growth <= LIMIT) & (growth_cols <= LIMIT)
        flag = jnp.broadcast_to(jnp.where(good, 0.0, 1.0), (1, RANK))
        stats = jnp.concatenate([squares, flag, jnp.zeros((6, RANK), f32)], axis=0)
        for i in range(DEPTHS):
            stats_ref[i] = stats

    square = jax.ShapeDtypeStruct((RANK, RANK), bf16)
    return pl.pallas_call(
        kernel,
        out_shape=(square, square, jax.ShapeDtypeStruct((DEPTHS, 8, RANK), f32)),
        in_specs=[SCALAR] + in_vmem(5),
        out_specs=tuple(in_vmem(3)),
        scratch_shapes=[pltpu.VMEM((2, QUARTER // 2, RANK), f32)],
        compiler_params=PARAMS,
    )(core, mine, other, upper, diagonal_upper, moment)


BLOCKS = tuple((low, min(low + 512, COLS)) for low in range(0, COLS, 512))
HBM = pl.BlockSpec(memory_space=pltpu.HBM)


def columns_and_momentum(core, mine, other, high, low, products, momentum, grad):
    def kernel(
        core_ref, mine_ref, other_ref, high_ref, low_ref, products_ref, momentum_hbm, grad_hbm,
        cols_ref, left_ref, new_hbm, wide_ref, full_ref, momentum_ref, grad_ref, new_ref, sems,
    ):
        loads = []
        for i, (begin, end) in enumerate(BLOCKS):
            cut = pl.ds(begin, end - begin)
            two = (
                pltpu.make_async_copy(
                    momentum_hbm.at[:, cut], momentum_ref.at[:, cut], sems.at[0, i]
                ),
                pltpu.make_async_copy(grad_hbm.at[:, cut], grad_ref.at[:, cut], sems.at[1, i]),
            )
            for load in two:
                load.start()
            loads.append(two)
        high, low = high_ref[...], low_ref[...]
        products = products_ref[...]
        left = (plain_dot(products, high, (1, 1)) + plain_dot(products, low, (1, 1))).astype(bf16)
        left_ref[...] = left
        for ref, half in ((mine_ref, core_ref[0]), (other_ref, 1 - core_ref[0])):
            rows = ref[...].reshape(PEERS * PACK, RANK)
            wide_ref[...] = plain_dot(rows, high, (1, 1)) + plain_dot(rows, low, (1, 1))
            for i in range(PEERS):
                start = pl.multiple_of(half * HALF + SHARE * i, 8)
                full_ref[pl.ds(start, SHARE), :] = wide_ref[PACK * i : PACK * i + SHARE, :]
        copies = []
        for i, (begin, end) in enumerate(BLOCKS):
            cols = full_ref[begin:end, :].astype(bf16)
            cols_ref[begin:end, :] = cols
            for load in loads[i]:
                load.wait()
            buffer = (
                momentum_ref[:, begin:end].astype(f32) + grad_ref[:, begin:end].astype(f32)
            ).astype(bf16)
            new_ref[:, begin:end] = (
                buffer.astype(f32) - (1.0 - keep_rate) / D * plain_dot(left, cols, (1, 1))
            ).astype(bf16)
            cut = pl.ds(begin, end - begin)
            copy = pltpu.make_async_copy(new_ref.at[:, cut], new_hbm.at[:, cut], sems.at[2, i])
            copy.start()
            copies.append(copy)
        for copy in copies:
            copy.wait()

    return pl.pallas_call(
        kernel,
        out_shape=(
            jax.ShapeDtypeStruct((COLS, RANK), bf16),
            jax.ShapeDtypeStruct((ROWS, RANK), bf16),
            jax.ShapeDtypeStruct((ROWS, COLS), bf16),
        ),
        in_specs=[SCALAR] + in_vmem(5) + [HBM, HBM],
        out_specs=(*in_vmem(2), HBM),
        scratch_shapes=[
            pltpu.VMEM((PEERS * PACK, RANK), f32),
            pltpu.VMEM((COLS, RANK), f32),
            pltpu.VMEM((ROWS, COLS), bf16),
            pltpu.VMEM((ROWS, COLS), bf16),
            pltpu.VMEM((ROWS, COLS), bf16),
            pltpu.SemaphoreType.DMA((3, len(BLOCKS))),
        ],
        compiler_params=PARAMS,
        cost_estimate=pl.CostEstimate(flops=5 * 10**9, bytes_accessed=10**6, transcendentals=0),
    )(core, mine, other, high, low, products, momentum, grad)


def factor_and_weight(stats, cols, left, weight):
    def kernel(
        stats_ref, cols_ref, left_ref, weight_hbm, factor_hbm, new_hbm, flag_ref,
        weight_ref, factor_ref, new_ref, sems,
    ):
        loads = []
        for i, (begin, end) in enumerate(BLOCKS):
            cut = pl.ds(begin, end - begin)
            load = pltpu.make_async_copy(
                weight_hbm.at[:, cut], weight_ref.at[:, cut], sems.at[0, i]
            )
            load.start()
            loads.append(load)
        total = stats_ref[0]
        for i in range(1, DEPTHS):
            total = total + stats_ref[i]
        inverse = lax.rsqrt(total[0:1, :] / FF + epsilon)
        flag_ref[0] = (jnp.max(total[1:2, :]) > 0.5).astype(jnp.int32)
        left = left_ref[...]
        copies = []
        for i, (begin, end) in enumerate(BLOCKS):
            cut = pl.ds(begin, end - begin)
            factor = (cols_ref[begin:end, :].astype(f32) * inverse).astype(bf16)
            factor_ref[begin:end, :] = factor
            copy = pltpu.make_async_copy(
                factor_ref.at[cut, :], factor_hbm.at[cut, :], sems.at[1, i]
            )
            copy.start()
            copies.append(copy)
            loads[i].wait()
            new_ref[:, begin:end] = (
                weight_ref[:, begin:end].astype(f32)
                - step_rate / math.sqrt(RANK) * plain_dot(left, factor, (1, 1))
            ).astype(bf16)
            copy = pltpu.make_async_copy(new_ref.at[:, cut], new_hbm.at[:, cut], sems.at[2, i])
            copy.start()
            copies.append(copy)
        for copy in copies:
            copy.wait()

    return pl.pallas_call(
        kernel,
        out_shape=(
            jax.ShapeDtypeStruct((COLS, RANK), bf16),
            jax.ShapeDtypeStruct((ROWS, COLS), bf16),
            jax.ShapeDtypeStruct((1,), jnp.int32),
        ),
        in_specs=in_vmem(3) + [HBM],
        out_specs=(HBM, HBM, SCALAR),
        scratch_shapes=[
            pltpu.VMEM((ROWS, COLS), bf16),
            pltpu.VMEM((COLS, RANK), bf16),
            pltpu.VMEM((ROWS, COLS), bf16),
            pltpu.SemaphoreType.DMA((3, len(BLOCKS))),
        ],
        compiler_params=PARAMS,
    )(stats, cols, left, weight)


def careful(weight, momentum, grad, q_factor):
    core = lax.axis_index(CORE)
    buffer = (momentum.astype(f32) + grad.astype(f32)).astype(bf16)
    partial_value = jnp.dot(buffer, q_factor, preferred_element_type=f32)
    products = gather(scatter_sum(partial_value, DEPTH, DEPTHS), DEPTH, DEPTHS)
    products = products.reshape(ROWS, RANK)
    gram = exact_dot(products, products, (0, 0))
    gram = gram + swap_core(gram)
    gram = gather(scatter_sum(gram, PLANE, PEERS), PLANE, PEERS).reshape(RANK, RANK)
    inverse = cholesky_inverse(gram)
    left_factor = (math.sqrt(D) * exact_dot(products, inverse, (1, 1))).astype(bf16)
    col_partial = plain_dot(buffer, left_factor, (0, 0))
    mine = lax.dynamic_slice_in_dim(col_partial, core * HALF, HALF, 0)
    theirs = lax.dynamic_slice_in_dim(col_partial, (1 - core) * HALF, HALF, 0)
    share = scatter_sum(mine + swap_core(theirs), PLANE, PEERS)
    squares = jnp.sum(gather(jnp.sum(share * share, axis=0)[None], EVERY, 256), axis=(0, 1))
    normalized = (share * lax.rsqrt(squares / FF + epsilon)).astype(bf16)
    mine = gather(normalized, PLANE, PEERS).reshape(HALF, RANK)
    new_factor = in_order(core, mine, swap_core(mine))
    scaled = (left_factor.astype(f32) * jnp.sqrt(squares / FF + epsilon)).astype(bf16)
    feedback = plain_dot(scaled, new_factor, (1, 1))
    new_momentum = (buffer.astype(f32) - (1.0 - keep_rate) / D * feedback).astype(bf16)
    update = plain_dot(left_factor, new_factor, (1, 1))
    new_weight = (weight.astype(f32) - step_rate / math.sqrt(RANK) * update).astype(bf16)
    return (new_weight, new_momentum, new_factor)


def on_device(weight, momentum, grad, q_factor):
    core = lax.axis_index(CORE).astype(jnp.int32).reshape(1)
    buffer, partial_value = buffer_and_products(momentum, grad, q_factor)
    parts = exchange(partial_value.reshape(DEPTHS, ROWS // DEPTHS, RANK), DEPTH)
    products = exchange(sum_products(parts), DEPTH).reshape(ROWS, RANK)

    gram, theirs = first_shares(core, buffer, products)
    gram_other, theirs = swap_core(gram), swap_core(theirs)
    mine = second_share(core, buffer, products)
    parts = exchange(pack_shares(core, mine, theirs, gram, gram_other), PLANE)
    mine = exchange(sum_shares(parts), PLANE)
    other = swap_core(mine)
    upper, diagonal_upper, moment = first_factor(mine)
    high, low, stats = second_factor(core, mine, other, upper, diagonal_upper, moment)
    stats = exchange(stats, DEPTH)
    cols, left, new_momentum = columns_and_momentum(
        core, mine, other, high, low, products, momentum, grad
    )
    new_factor, new_weight, flag = factor_and_weight(stats, cols, left, weight)

    def again(state):
        return (jnp.zeros((1,), jnp.int32), *careful(weight, momentum, grad, q_factor))

    state = lax.while_loop(
        lambda state: state[0][0] > 0, again, (flag, new_weight, new_momentum, new_factor)
    )
    return state[1:]


def solution(mesh):
    fine = Mesh(mesh.devices.reshape(4, 4, 2, 8), EVERY)
    rows = ("x", "y", CORE)
    placed = (P(rows, DEPTH), P(rows, DEPTH), P(rows, DEPTH), P(DEPTH, None))
    return jax.shard_map(
        on_device,
        mesh=fine,
        in_specs=placed,
        out_specs=(P(rows, DEPTH), P(rows, DEPTH), P(DEPTH, None)),
        check_vma=False,
    )
```

```python
import math

import jax
import jax.numpy as jnp
from jax import lax
from jax.experimental import pallas as pl
from jax.experimental.pallas import tpu as pltpu
from jax.sharding import Mesh, PartitionSpec as P

D = 8192
FF = 26624
RANK = 256

epsilon = 1e-06
keep_rate = 0.9
step_rate = 0.5

HIGHEST = lax.Precision.HIGHEST
f32 = jnp.float32
bf16 = jnp.bfloat16

CORE = "core"
PLANE = ("x", "y")
DEPTH = "z"
EVERY = ("x", "y", "core", "z")

ROWS = 256
COLS = 3328
HALF = 1664
PEERS = 16
SHARE = 104
GRAM = 8
QUARTER = 128
PACK = 120
TILES = 112
DEPTHS = 8
LIMIT = 4.0


def exact_dot(a, b, contract):
    dims = (((contract[0],), (contract[1],)), ((), ()))
    return lax.dot_general(a, b, dims, precision=HIGHEST, preferred_element_type=f32)


def plain_dot(a, b, contract):
    dims = (((contract[0],), (contract[1],)), ((), ()))
    return lax.dot_general(a, b, dims, preferred_element_type=f32)


def in_vmem(count):
    return [pl.BlockSpec(memory_space=pltpu.VMEM)] * count


SCALAR = pl.BlockSpec(memory_space=pltpu.SMEM)
PARAMS = pltpu.CompilerParams(vmem_limit_bytes=20 * 2**20)


LEAF = 64
PANEL = 16


def leaf_inverse(a):
    n = a.shape[0]
    lanes = 2 * n
    rows = lax.broadcasted_iota(jnp.int32, (n, n), 0)
    cols = lax.broadcasted_iota(jnp.int32, (n, n), 1)
    eye = (rows == cols).astype(f32)
    both = jnp.concatenate([a, eye], axis=1)
    count = n // 8
    slabs = [both[8 * i : 8 * i + 8, :] for i in range(count)]
    row8 = lax.broadcasted_iota(jnp.int32, (8, lanes), 0)
    for first in range(0, count, PANEL // 8):
        panel = [
            [
                jnp.broadcast_to(slabs[i][:, 8 * first + k : 8 * first + k + 1], (8, lanes))
                for i in range(first, count)
            ]
            for k in range(PANEL)
        ]
        for k in range(PANEL):
            at, sub = first + k // 8, k % 8
            pivot = jnp.broadcast_to(panel[k][at - first][sub : sub + 1, :], (8, lanes))
            inverse = 1.0 / pivot
            factor = {}
            for i in range(at, count):
                value = panel[k][i - first] * inverse
                factor[i] = jnp.where(row8 > sub, value, 0.0) if i == at else value
            for m in range(k + 1, PANEL):
                row = jnp.broadcast_to(panel[m][at - first][sub : sub + 1, :], (8, lanes))
                for i in range(at, count):
                    panel[m][i - first] = panel[m][i - first] - factor[i] * row
            row = jnp.broadcast_to(slabs[at][sub : sub + 1, :], (8, lanes))
            for i in range(at, count):
                slabs[i] = slabs[i] - factor[i] * row
    both = jnp.concatenate(slabs, axis=0)
    pivots = jnp.sum(both[:, :n] * eye, axis=1, keepdims=True)
    return both[:, n:] * lax.rsqrt(pivots)


def triangle_inverse(a):
    n = a.shape[0]
    if n <= LEAF:
        return leaf_inverse(a)
    h = n // 2
    upper = triangle_inverse(a[:h, :h])
    below = exact_dot(a[h:, :h], upper, (1, 1))
    rest = a[h:, h:] - exact_dot(below, below, (1, 1))
    mixed = exact_dot(below, upper, (1, 0))
    lower = triangle_inverse(rest)
    corner = -exact_dot(lower, mixed, (1, 0))
    top = jnp.concatenate([upper, jnp.zeros((h, n - h), f32)], axis=1)
    return jnp.concatenate([top, jnp.concatenate([corner, lower], axis=1)], axis=0)


def cholesky_inverse(gram):
    def kernel(gram_ref, inverse_ref):
        inverse_ref[...] = triangle_inverse(gram_ref[...])

    return pl.pallas_call(
        kernel,
        out_shape=jax.ShapeDtypeStruct((RANK, RANK), f32),
        in_specs=in_vmem(1),
        out_specs=in_vmem(1)[0],
        compiler_params=PARAMS,
    )(gram)


def exchange(pieces, axis):
    return lax.all_to_all(pieces, axis, 0, 0)


def scatter_sum(value, axis, parts):
    pieces = value.reshape(parts, value.shape[0] // parts, *value.shape[1:])
    return jnp.sum(exchange(pieces, axis).astype(f32), axis=0)


def gather(value, axis, parts):
    return exchange(jnp.broadcast_to(value[None], (parts, *value.shape)), axis)


def swap_core(value):
    return lax.ppermute(value, CORE, [(0, 1), (1, 0)])


def in_order(core, mine, other):
    first = core == 0
    return jnp.concatenate([jnp.where(first, mine, other), jnp.where(first, other, mine)], axis=0)


def guarded(total, energy, rows):
    size = jnp.sum(total[:rows] * total[:rows], axis=0, keepdims=True)
    growth = jnp.sum(energy / size, axis=1, keepdims=True) * (1.0 / RANK)
    return jnp.where(growth <= LIMIT, total, jnp.nan)


def split(value):
    high = value.astype(bf16).astype(f32)
    return high, value - high


CUTS = (0, 1664, 3328)


def buffer_and_products(momentum, grad, q_factor):
    def kernel(
        momentum_hbm, grad_hbm, q_hbm, buffer_ref, out_ref, momentum_ref, grad_ref, q_ref, sems
    ):
        copies = []
        for i, (low, high) in enumerate(zip(CUTS[:-1], CUTS[1:])):
            cut = pl.ds(low, high - low)
            three = (
                pltpu.make_async_copy(momentum_hbm.at[:, cut], momentum_ref.at[:, cut], sems.at[i, 0]),
                pltpu.make_async_copy(grad_hbm.at[:, cut], grad_ref.at[:, cut], sems.at[i, 1]),
                pltpu.make_async_copy(q_hbm.at[cut, :], q_ref.at[cut, :], sems.at[i, 2]),
            )
            for copy in three:
                copy.start()
            copies.append(three)
        total = jnp.zeros((ROWS, RANK), f32)
        for (low, high), three in zip(zip(CUTS[:-1], CUTS[1:]), copies):
            for copy in three:
                copy.wait()
            part = (
                momentum_ref[:, low:high].astype(f32) + grad_ref[:, low:high].astype(f32)
            ).astype(bf16)
            buffer_ref[:, low:high] = part
            total = total + plain_dot(part, q_ref[low:high, :], (1, 0))
        out_ref[...] = total.astype(bf16)

    return pl.pallas_call(
        kernel,
        out_shape=(
            jax.ShapeDtypeStruct((ROWS, COLS), bf16),
            jax.ShapeDtypeStruct((ROWS, RANK), bf16),
        ),
        in_specs=[pl.BlockSpec(memory_space=pltpu.HBM)] * 3,
        out_specs=tuple(in_vmem(2)),
        scratch_shapes=[
            pltpu.VMEM((ROWS, COLS), bf16),
            pltpu.VMEM((ROWS, COLS), bf16),
            pltpu.VMEM((COLS, RANK), bf16),
            pltpu.SemaphoreType.DMA((len(CUTS) - 1, 3)),
        ],
        compiler_params=PARAMS,
    )(momentum, grad, q_factor)


def sum_products(parts):
    def kernel(parts_ref, out_ref):
        total = jnp.zeros((ROWS // DEPTHS, RANK), f32)
        energy = jnp.zeros((1, RANK), f32)
        for i in range(DEPTHS):
            part = parts_ref[i].astype(f32)
            total = total + part
            energy = energy + jnp.sum(part * part, axis=0, keepdims=True)
        total = guarded(total, energy, ROWS // DEPTHS).astype(bf16)
        for i in range(DEPTHS):
            out_ref[i] = total

    return pl.pallas_call(
        kernel,
        out_shape=jax.ShapeDtypeStruct(parts.shape, bf16),
        in_specs=in_vmem(1),
        out_specs=in_vmem(1)[0],
        compiler_params=PARAMS,
    )(parts)


def first_shares(core, buffer, products):
    def kernel(core_ref, buffer_ref, products_ref, gram_ref, theirs_ref):
        products = products_ref[...]
        start = pl.multiple_of((1 - core_ref[0]) * HALF, 128)
        theirs_ref[...] = plain_dot(buffer_ref[:, pl.ds(start, HALF)], products, (0, 0)).astype(bf16)
        gram_ref[...] = plain_dot(products, products, (0, 0))

    return pl.pallas_call(
        kernel,
        out_shape=(
            jax.ShapeDtypeStruct((RANK, RANK), f32),
            jax.ShapeDtypeStruct((HALF, RANK), bf16),
        ),
        in_specs=[SCALAR] + in_vmem(2),
        out_specs=tuple(in_vmem(2)),
        compiler_params=PARAMS,
    )(core, buffer, products)


def second_share(core, buffer, products):
    def kernel(core_ref, buffer_ref, products_ref, mine_ref):
        start = pl.multiple_of(core_ref[0] * HALF, 128)
        mine_ref[...] = plain_dot(buffer_ref[:, pl.ds(start, HALF)], products_ref[...], (0, 0))

    return pl.pallas_call(
        kernel,
        out_shape=jax.ShapeDtypeStruct((HALF, RANK), f32),
        in_specs=[SCALAR] + in_vmem(2),
        out_specs=in_vmem(1)[0],
        compiler_params=PARAMS,
    )(core, buffer, products)


def pack_shares(core, mine, theirs, gram, gram_other):
    def kernel(core_ref, mine_ref, theirs_ref, gram_ref, other_ref, out_ref):
        start = pl.multiple_of(core_ref[0] * (QUARTER // 2) + QUARTER, 8)
        energy = jnp.zeros((1, RANK), f32)
        size = jnp.zeros((1, RANK), f32)
        for i in range(PEERS):
            one = mine_ref[SHARE * i : SHARE * (i + 1), :]
            two = theirs_ref[SHARE * i : SHARE * (i + 1), :].astype(f32)
            both = one + two
            energy = energy + jnp.sum(one * one + two * two, axis=0, keepdims=True)
            size = size + jnp.sum(both * both, axis=0, keepdims=True)
            upper = slice(GRAM * i, GRAM * (i + 1))
            upper = gram_ref[upper, :QUARTER] + other_ref[upper, :QUARTER]
            lower = pl.ds(start + GRAM * (i // 2), GRAM)
            lower = gram_ref[lower, :] + other_ref[lower, :]
            lower = lower[4 * (i % 2) : 4 * (i % 2) + 4, :]
            lower = jnp.concatenate([lower[:, :QUARTER], lower[:, QUARTER:]], axis=0)
            parts = split(jnp.concatenate([upper, lower], axis=1))
            out_ref[i] = jnp.concatenate([both, *parts], axis=0).astype(bf16)
        growth = jnp.sum(energy / size, axis=1, keepdims=True) * (1.0 / RANK)

        @pl.when(jnp.logical_not(jnp.max(growth) <= LIMIT))
        def _():
            out_ref[...] = jnp.full(out_ref.shape, jnp.nan, bf16)

    return pl.pallas_call(
        kernel,
        out_shape=jax.ShapeDtypeStruct((PEERS, PACK, RANK), bf16),
        in_specs=[SCALAR] + in_vmem(4),
        out_specs=in_vmem(1)[0],
        compiler_params=PARAMS,
    )(core, mine, theirs, gram, gram_other)


def sum_shares(parts):
    def kernel(parts_ref, out_ref):
        total = jnp.zeros((PACK, RANK), f32)
        energy = jnp.zeros((1, RANK), f32)
        for i in range(PEERS):
            part = parts_ref[i].astype(f32)
            total = total + part
            energy = energy + jnp.sum(part[:SHARE] * part[:SHARE], axis=0, keepdims=True)
        total = guarded(total, energy, SHARE)
        gram = total[SHARE : SHARE + GRAM] + total[SHARE + GRAM :]
        packed = jnp.concatenate([total[:SHARE], *split(gram)], axis=0).astype(bf16)
        for i in range(PEERS):
            out_ref[i] = packed

    return pl.pallas_call(
        kernel,
        out_shape=jax.ShapeDtypeStruct(parts.shape, bf16),
        in_specs=in_vmem(1),
        out_specs=in_vmem(1)[0],
        compiler_params=PARAMS,
    )(parts)


def gram_block(ref, i):
    block = ref[i].astype(f32)
    return block[SHARE : SHARE + GRAM] + block[SHARE + GRAM :]


def second_moment(ref):
    full = TILES - 16
    rows = []
    keep = lax.broadcasted_iota(jnp.int32, (16, RANK), 0) < SHARE - full
    for i in range(PEERS):
        last = jnp.where(keep, ref[i, full:TILES, :].astype(f32), 0.0).astype(bf16)
        rows += [ref[i, :full, :], last]
    rows = jnp.concatenate(rows, axis=0)
    return plain_dot(rows, rows, (0, 0))


def diagonal(value):
    n = value.shape[0]
    rows = lax.broadcasted_iota(jnp.int32, (n, n), 0)
    cols = lax.broadcasted_iota(jnp.int32, (n, n), 1)
    return jnp.sum(jnp.where(rows == cols, value, 0.0), axis=0, keepdims=True)


def as_row(column):
    return diagonal(jnp.broadcast_to(column, (column.shape[0], column.shape[0])))


def first_factor(mine):
    def kernel(mine_ref, upper_ref, diagonal_ref, moment_ref):
        gram = jnp.concatenate(
            [gram_block(mine_ref, i)[:, :QUARTER] for i in range(PEERS)], axis=0
        )
        upper_ref[...] = triangle_inverse(gram)
        diagonal_ref[...] = jnp.broadcast_to(diagonal(gram), (8, QUARTER))
        moment_ref[...] = second_moment(mine_ref)

    return pl.pallas_call(
        kernel,
        out_shape=(
            jax.ShapeDtypeStruct((QUARTER, QUARTER), f32),
            jax.ShapeDtypeStruct((8, QUARTER), f32),
            jax.ShapeDtypeStruct((RANK, RANK), f32),
        ),
        in_specs=in_vmem(1),
        out_specs=tuple(in_vmem(3)),
        compiler_params=PARAMS,
        cost_estimate=pl.CostEstimate(flops=10**10, bytes_accessed=10**6, transcendentals=0),
    )(mine)


def second_factor(core, mine, other, upper, diagonal_upper, moment):
    def kernel(
        core_ref, mine_ref, other_ref, upper_ref, diagonal_ref, moment_ref, high_ref, low_ref,
        stats_ref, rows_ref,
    ):
        for at, ref in enumerate((mine_ref, other_ref)):
            for i in range(PEERS):
                block = gram_block(ref, i)
                rows_ref[at, 4 * i : 4 * i + 4, :QUARTER] = block[:4, QUARTER:]
                rows_ref[at, 4 * i : 4 * i + 4, QUARTER:] = block[4:, QUARTER:]
        first = core_ref[0] == 0
        one, two = rows_ref[0], rows_ref[1]
        gram = jnp.concatenate([jnp.where(first, one, two), jnp.where(first, two, one)], axis=0)
        upper = upper_ref[...]
        below = exact_dot(gram[:, :QUARTER], upper, (1, 1))
        rest = gram[:, QUARTER:]
        mixed = exact_dot(below, upper, (1, 0))
        lower = triangle_inverse(rest - exact_dot(below, below, (1, 1)))
        corner = -exact_dot(lower, mixed, (1, 0))
        zeros = jnp.zeros((QUARTER, QUARTER), f32)
        inverse = jnp.concatenate(
            [
                jnp.concatenate([upper, zeros], axis=1),
                jnp.concatenate([corner, lower], axis=1),
            ],
            axis=0,
        )
        scaled = math.sqrt(D) * inverse
        high = scaled.astype(bf16)
        high_ref[...] = high
        low_ref[...] = (scaled - high.astype(f32)).astype(bf16)
        moment = moment_ref[...] + second_moment(other_ref)
        low = low_ref[...]
        moment_high = moment.astype(bf16)
        moment_low = (moment - moment_high.astype(f32)).astype(bf16)
        product = plain_dot(high, moment_high, (1, 0)) + (
            plain_dot(high, moment_low, (1, 0)) + plain_dot(low, moment_high, (1, 0))
        )
        squares = as_row(jnp.sum(product * scaled, axis=1, keepdims=True))
        gram_diagonal = jnp.concatenate([diagonal_ref[0:1, :], diagonal(rest)], axis=1)
        weights = jnp.sum(inverse * inverse, axis=0, keepdims=True)
        growth = jnp.sum(gram_diagonal * weights, axis=1, keepdims=True) * (1.0 / RANK)
        noise = as_row(jnp.sum(scaled * scaled * diagonal(moment), axis=1, keepdims=True))
        ratio = jnp.where(squares > 0.0, noise / squares, jnp.inf)
        growth_cols = jnp.sum(ratio, axis=1, keepdims=True) * (1.0 / RANK)
        good = (growth <= LIMIT) & (growth_cols <= LIMIT)
        flag = jnp.broadcast_to(jnp.where(good, 0.0, 1.0), (1, RANK))
        stats = jnp.concatenate([squares, flag, jnp.zeros((6, RANK), f32)], axis=0)
        for i in range(DEPTHS):
            stats_ref[i] = stats

    square = jax.ShapeDtypeStruct((RANK, RANK), bf16)
    return pl.pallas_call(
        kernel,
        out_shape=(square, square, jax.ShapeDtypeStruct((DEPTHS, 8, RANK), f32)),
        in_specs=[SCALAR] + in_vmem(5),
        out_specs=tuple(in_vmem(3)),
        scratch_shapes=[pltpu.VMEM((2, QUARTER // 2, RANK), f32)],
        compiler_params=PARAMS,
    )(core, mine, other, upper, diagonal_upper, moment)


BLOCKS = ((0, 1664), (1664, 3328))
HBM = pl.BlockSpec(memory_space=pltpu.HBM)


def columns_and_momentum(core, mine, other, high, low, products, momentum, grad):
    def kernel(
        core_ref, mine_ref, other_ref, high_ref, low_ref, products_ref, momentum_hbm, grad_hbm,
        cols_ref, left_ref, new_hbm, momentum_ref, grad_ref, new_ref, sems,
    ):
        loads = []
        for i, (begin, end) in enumerate(BLOCKS):
            cut = pl.ds(begin, end - begin)
            two = (
                pltpu.make_async_copy(
                    momentum_hbm.at[:, cut], momentum_ref.at[:, cut], sems.at[0, i]
                ),
                pltpu.make_async_copy(grad_hbm.at[:, cut], grad_ref.at[:, cut], sems.at[1, i]),
            )
            for load in two:
                load.start()
            loads.append(two)
        high, low = high_ref[...], low_ref[...]
        products = products_ref[...]
        left = (plain_dot(products, high, (1, 1)) + plain_dot(products, low, (1, 1))).astype(bf16)
        left_ref[...] = left
        for ref, half in ((mine_ref, core_ref[0]), (other_ref, 1 - core_ref[0])):
            rows = jnp.concatenate([ref[i, :TILES, :] for i in range(PEERS)], axis=0)
            wide = plain_dot(rows, high, (1, 1)) + plain_dot(rows, low, (1, 1))
            for i in range(0, PEERS, 2):
                one = wide[TILES * i : TILES * i + SHARE, :]
                two = wide[TILES * (i + 1) : TILES * (i + 1) + SHARE, :]
                start = pl.multiple_of(half * HALF + SHARE * i, 16)
                pair = jnp.concatenate([one, two], axis=0).astype(bf16)
                cols_ref[pl.ds(start, 2 * SHARE), :] = pair
        copies = []
        for i, (begin, end) in enumerate(BLOCKS):
            cols = cols_ref[begin:end, :]
            for load in loads[i]:
                load.wait()
            buffer = (
                momentum_ref[:, begin:end].astype(f32) + grad_ref[:, begin:end].astype(f32)
            ).astype(bf16)
            new_ref[:, begin:end] = (
                buffer.astype(f32) - (1.0 - keep_rate) / D * plain_dot(left, cols, (1, 1))
            ).astype(bf16)
            cut = pl.ds(begin, end - begin)
            copy = pltpu.make_async_copy(new_ref.at[:, cut], new_hbm.at[:, cut], sems.at[2, i])
            copy.start()
            copies.append(copy)
        for copy in copies:
            copy.wait()

    return pl.pallas_call(
        kernel,
        out_shape=(
            jax.ShapeDtypeStruct((COLS, RANK), bf16),
            jax.ShapeDtypeStruct((ROWS, RANK), bf16),
            jax.ShapeDtypeStruct((ROWS, COLS), bf16),
        ),
        in_specs=[SCALAR] + in_vmem(5) + [HBM, HBM],
        out_specs=(*in_vmem(2), HBM),
        scratch_shapes=[
            pltpu.VMEM((ROWS, COLS), bf16),
            pltpu.VMEM((ROWS, COLS), bf16),
            pltpu.VMEM((ROWS, COLS), bf16),
            pltpu.SemaphoreType.DMA((3, len(BLOCKS))),
        ],
        compiler_params=PARAMS,
        cost_estimate=pl.CostEstimate(flops=5 * 10**9, bytes_accessed=10**6, transcendentals=0),
    )(core, mine, other, high, low, products, momentum, grad)


def factor_and_weight(stats, cols, left, weight):
    def kernel(
        stats_ref, cols_ref, left_ref, weight_hbm, factor_hbm, new_hbm, flag_ref,
        weight_ref, factor_ref, new_ref, sems, sem_factor,
    ):
        loads = []
        for i, (begin, end) in enumerate(BLOCKS):
            cut = pl.ds(begin, end - begin)
            load = pltpu.make_async_copy(
                weight_hbm.at[:, cut], weight_ref.at[:, cut], sems.at[0, i]
            )
            load.start()
            loads.append(load)
        total = stats_ref[0]
        for i in range(1, DEPTHS):
            total = total + stats_ref[i]
        inverse = lax.rsqrt(total[0:1, :] / FF + epsilon)
        flag_ref[0] = (jnp.max(total[1:2, :]) > 0.5).astype(jnp.int32)
        factor_ref[...] = (cols_ref[...].astype(f32) * inverse).astype(bf16)
        copies = [pltpu.make_async_copy(factor_ref, factor_hbm, sem_factor.at[0])]
        copies[0].start()
        left = left_ref[...]
        for i, (begin, end) in enumerate(BLOCKS):
            cut = pl.ds(begin, end - begin)
            loads[i].wait()
            new_ref[:, begin:end] = (
                weight_ref[:, begin:end].astype(f32)
                - step_rate / math.sqrt(RANK) * plain_dot(left, factor_ref[begin:end, :], (1, 1))
            ).astype(bf16)
            copy = pltpu.make_async_copy(new_ref.at[:, cut], new_hbm.at[:, cut], sems.at[1, i])
            copy.start()
            copies.append(copy)
        for copy in copies:
            copy.wait()

    return pl.pallas_call(
        kernel,
        out_shape=(
            jax.ShapeDtypeStruct((COLS, RANK), bf16),
            jax.ShapeDtypeStruct((ROWS, COLS), bf16),
            jax.ShapeDtypeStruct((1,), jnp.int32),
        ),
        in_specs=in_vmem(3) + [HBM],
        out_specs=(HBM, HBM, SCALAR),
        scratch_shapes=[
            pltpu.VMEM((ROWS, COLS), bf16),
            pltpu.VMEM((COLS, RANK), bf16),
            pltpu.VMEM((ROWS, COLS), bf16),
            pltpu.SemaphoreType.DMA((2, len(BLOCKS))),
            pltpu.SemaphoreType.DMA((1,)),
        ],
        compiler_params=PARAMS,
    )(stats, cols, left, weight)


def careful(weight, momentum, grad, q_factor):
    core = lax.axis_index(CORE)
    buffer = (momentum.astype(f32) + grad.astype(f32)).astype(bf16)
    partial_value = jnp.dot(buffer, q_factor, preferred_element_type=f32)
    products = gather(scatter_sum(partial_value, DEPTH, DEPTHS), DEPTH, DEPTHS)
    products = products.reshape(ROWS, RANK)
    gram = exact_dot(products, products, (0, 0))
    gram = gram + swap_core(gram)
    gram = gather(scatter_sum(gram, PLANE, PEERS), PLANE, PEERS).reshape(RANK, RANK)
    inverse = cholesky_inverse(gram)
    left_factor = (math.sqrt(D) * exact_dot(products, inverse, (1, 1))).astype(bf16)
    col_partial = plain_dot(buffer, left_factor, (0, 0))
    mine = lax.dynamic_slice_in_dim(col_partial, core * HALF, HALF, 0)
    theirs = lax.dynamic_slice_in_dim(col_partial, (1 - core) * HALF, HALF, 0)
    share = scatter_sum(mine + swap_core(theirs), PLANE, PEERS)
    squares = jnp.sum(gather(jnp.sum(share * share, axis=0)[None], EVERY, 256), axis=(0, 1))
    normalized = (share * lax.rsqrt(squares / FF + epsilon)).astype(bf16)
    mine = gather(normalized, PLANE, PEERS).reshape(HALF, RANK)
    new_factor = in_order(core, mine, swap_core(mine))
    scaled = (left_factor.astype(f32) * jnp.sqrt(squares / FF + epsilon)).astype(bf16)
    feedback = plain_dot(scaled, new_factor, (1, 1))
    new_momentum = (buffer.astype(f32) - (1.0 - keep_rate) / D * feedback).astype(bf16)
    update = plain_dot(left_factor, new_factor, (1, 1))
    new_weight = (weight.astype(f32) - step_rate / math.sqrt(RANK) * update).astype(bf16)
    return (new_weight, new_momentum, new_factor)


def on_device(weight, momentum, grad, q_factor):
    core = lax.axis_index(CORE).astype(jnp.int32).reshape(1)
    buffer, partial_value = buffer_and_products(momentum, grad, q_factor)
    parts = exchange(partial_value.reshape(DEPTHS, ROWS // DEPTHS, RANK), DEPTH)
    products = exchange(sum_products(parts), DEPTH).reshape(ROWS, RANK)

    gram, theirs = first_shares(core, buffer, products)
    gram_other, theirs = swap_core(gram), swap_core(theirs)
    mine = second_share(core, buffer, products)
    parts = exchange(pack_shares(core, mine, theirs, gram, gram_other), PLANE)
    mine = exchange(sum_shares(parts), PLANE)
    other = swap_core(mine)
    upper, diagonal_upper, moment = first_factor(mine)
    high, low, stats = second_factor(core, mine, other, upper, diagonal_upper, moment)
    stats = exchange(stats, DEPTH)
    cols, left, new_momentum = columns_and_momentum(
        core, mine, other, high, low, products, momentum, grad
    )
    new_factor, new_weight, flag = factor_and_weight(stats, cols, left, weight)

    def again(state):
        return (jnp.zeros((1,), jnp.int32), *careful(weight, momentum, grad, q_factor))

    state = lax.while_loop(
        lambda state: state[0][0] > 0, again, (flag, new_weight, new_momentum, new_factor)
    )
    return state[1:]


def solution(mesh):
    fine = Mesh(mesh.devices.reshape(4, 4, 2, 8), EVERY)
    rows = ("x", "y", CORE)
    placed = (P(rows, DEPTH), P(rows, DEPTH), P(rows, DEPTH), P(DEPTH, None))
    return jax.shard_map(
        on_device,
        mesh=fine,
        in_specs=placed,
        out_specs=(P(rows, DEPTH), P(rows, DEPTH), P(DEPTH, None)),
        check_vma=False,
    )
```

```python
import math

import jax
import jax.numpy as jnp
from jax import lax
from jax.experimental import pallas as pl
from jax.experimental.pallas import tpu as pltpu
from jax.sharding import Mesh, PartitionSpec as P

D = 8192
FF = 26624
RANK = 256

epsilon = 1e-06
keep_rate = 0.9
step_rate = 0.5

HIGHEST = lax.Precision.HIGHEST
f32 = jnp.float32
bf16 = jnp.bfloat16

CORE = "core"
PLANE = ("x", "y")
DEPTH = "z"
EVERY = ("x", "y", "core", "z")

ROWS = 256
COLS = 3328
HALF = 1664
PEERS = 16
SHARE = 104
GRAM = 8
QUARTER = 128
PACK = 120
TILES = 112
DEPTHS = 8
LIMIT = 4.0


def exact_dot(a, b, contract):
    dims = (((contract[0],), (contract[1],)), ((), ()))
    return lax.dot_general(a, b, dims, precision=HIGHEST, preferred_element_type=f32)


def plain_dot(a, b, contract):
    dims = (((contract[0],), (contract[1],)), ((), ()))
    return lax.dot_general(a, b, dims, preferred_element_type=f32)


def two_parts(value):
    high = value.astype(bf16)
    return high, (value - high.astype(f32)).astype(bf16)


def close_dot(a, b, contract):
    a_high, a_low = two_parts(a)
    b_high, b_low = two_parts(b)
    return plain_dot(a_high, b_high, contract) + (
        plain_dot(a_high, b_low, contract) + plain_dot(a_low, b_high, contract)
    )


def in_vmem(count):
    return [pl.BlockSpec(memory_space=pltpu.VMEM)] * count


SCALAR = pl.BlockSpec(memory_space=pltpu.SMEM)
PARAMS = pltpu.CompilerParams(vmem_limit_bytes=20 * 2**20)


LEAF = 64
PANEL = 16


def leaf_inverse(a):
    n = a.shape[0]
    lanes = 2 * n
    rows = lax.broadcasted_iota(jnp.int32, (n, n), 0)
    cols = lax.broadcasted_iota(jnp.int32, (n, n), 1)
    eye = (rows == cols).astype(f32)
    both = jnp.concatenate([a, eye], axis=1)
    count = n // 8
    slabs = [both[8 * i : 8 * i + 8, :] for i in range(count)]
    row8 = lax.broadcasted_iota(jnp.int32, (8, lanes), 0)
    for first in range(0, count, PANEL // 8):
        panel = [
            [
                jnp.broadcast_to(slabs[i][:, 8 * first + k : 8 * first + k + 1], (8, lanes))
                for i in range(first, count)
            ]
            for k in range(PANEL)
        ]
        for k in range(PANEL):
            at, sub = first + k // 8, k % 8
            pivot = jnp.broadcast_to(panel[k][at - first][sub : sub + 1, :], (8, lanes))
            inverse = 1.0 / pivot
            factor = {}
            for i in range(at, count):
                value = panel[k][i - first] * inverse
                factor[i] = jnp.where(row8 > sub, value, 0.0) if i == at else value
            for m in range(k + 1, PANEL):
                row = jnp.broadcast_to(panel[m][at - first][sub : sub + 1, :], (8, lanes))
                for i in range(at, count):
                    panel[m][i - first] = panel[m][i - first] - factor[i] * row
            row = jnp.broadcast_to(slabs[at][sub : sub + 1, :], (8, lanes))
            for i in range(at, count):
                slabs[i] = slabs[i] - factor[i] * row
    both = jnp.concatenate(slabs, axis=0)
    pivots = jnp.sum(both[:, :n] * eye, axis=1, keepdims=True)
    return both[:, n:] * lax.rsqrt(pivots)


def triangle_inverse(a, dot=exact_dot):
    n = a.shape[0]
    if n <= LEAF:
        return leaf_inverse(a)
    h = n // 2
    upper = triangle_inverse(a[:h, :h], dot)
    below = dot(a[h:, :h], upper, (1, 1))
    rest = a[h:, h:] - dot(below, below, (1, 1))
    mixed = dot(below, upper, (1, 0))
    lower = triangle_inverse(rest, dot)
    corner = -dot(lower, mixed, (1, 0))
    top = jnp.concatenate([upper, jnp.zeros((h, n - h), f32)], axis=1)
    return jnp.concatenate([top, jnp.concatenate([corner, lower], axis=1)], axis=0)


def cholesky_inverse(gram):
    def kernel(gram_ref, inverse_ref):
        inverse_ref[...] = triangle_inverse(gram_ref[...])

    return pl.pallas_call(
        kernel,
        out_shape=jax.ShapeDtypeStruct((RANK, RANK), f32),
        in_specs=in_vmem(1),
        out_specs=in_vmem(1)[0],
        compiler_params=PARAMS,
    )(gram)


def exchange(pieces, axis):
    return lax.all_to_all(pieces, axis, 0, 0)


def scatter_sum(value, axis, parts):
    pieces = value.reshape(parts, value.shape[0] // parts, *value.shape[1:])
    return jnp.sum(exchange(pieces, axis).astype(f32), axis=0)


def gather(value, axis, parts):
    return exchange(jnp.broadcast_to(value[None], (parts, *value.shape)), axis)


def swap_core(value):
    return lax.ppermute(value, CORE, [(0, 1), (1, 0)])


def in_order(core, mine, other):
    first = core == 0
    return jnp.concatenate([jnp.where(first, mine, other), jnp.where(first, other, mine)], axis=0)


def guarded(total, energy, rows):
    size = jnp.sum(total[:rows] * total[:rows], axis=0, keepdims=True)
    growth = jnp.sum(energy / size, axis=1, keepdims=True) * (1.0 / RANK)
    return jnp.where(growth <= LIMIT, total, jnp.nan)


def split(value):
    high = value.astype(bf16).astype(f32)
    return high, value - high


CUTS = (0, 896, 1792, 2560, 3328)


def buffer_and_products(momentum, grad, q_factor):
    def kernel(
        momentum_hbm, grad_hbm, q_hbm, buffer_ref, out_ref, momentum_ref, grad_ref, q_ref, sems
    ):
        copies = []
        for i, (low, high) in enumerate(zip(CUTS[:-1], CUTS[1:])):
            cut = pl.ds(low, high - low)
            three = (
                pltpu.make_async_copy(momentum_hbm.at[:, cut], momentum_ref.at[:, cut], sems.at[i, 0]),
                pltpu.make_async_copy(grad_hbm.at[:, cut], grad_ref.at[:, cut], sems.at[i, 1]),
                pltpu.make_async_copy(q_hbm.at[cut, :], q_ref.at[cut, :], sems.at[i, 2]),
            )
            for copy in three:
                copy.start()
            copies.append(three)
        total = jnp.zeros((ROWS, RANK), f32)
        for (low, high), three in zip(zip(CUTS[:-1], CUTS[1:]), copies):
            for copy in three:
                copy.wait()
            part = (
                momentum_ref[:, low:high].astype(f32) + grad_ref[:, low:high].astype(f32)
            ).astype(bf16)
            buffer_ref[:, low:high] = part
            total = total + plain_dot(part, q_ref[low:high, :], (1, 0))
        out_ref[...] = total.astype(bf16)

    return pl.pallas_call(
        kernel,
        out_shape=(
            jax.ShapeDtypeStruct((ROWS, COLS), bf16),
            jax.ShapeDtypeStruct((ROWS, RANK), bf16),
        ),
        in_specs=[pl.BlockSpec(memory_space=pltpu.HBM)] * 3,
        out_specs=tuple(in_vmem(2)),
        scratch_shapes=[
            pltpu.VMEM((ROWS, COLS), bf16),
            pltpu.VMEM((ROWS, COLS), bf16),
            pltpu.VMEM((COLS, RANK), bf16),
            pltpu.SemaphoreType.DMA((len(CUTS) - 1, 3)),
        ],
        compiler_params=PARAMS,
    )(momentum, grad, q_factor)


def sum_products(parts):
    def kernel(parts_ref, out_ref):
        total = jnp.zeros((ROWS // DEPTHS, RANK), f32)
        energy = jnp.zeros((1, RANK), f32)
        for i in range(DEPTHS):
            part = parts_ref[i].astype(f32)
            total = total + part
            energy = energy + jnp.sum(part * part, axis=0, keepdims=True)
        total = guarded(total, energy, ROWS // DEPTHS).astype(bf16)
        for i in range(DEPTHS):
            out_ref[i] = total

    return pl.pallas_call(
        kernel,
        out_shape=jax.ShapeDtypeStruct(parts.shape, bf16),
        in_specs=in_vmem(1),
        out_specs=in_vmem(1)[0],
        compiler_params=PARAMS,
    )(parts)


def first_shares(core, buffer, products):
    def kernel(core_ref, buffer_ref, products_ref, gram_ref, theirs_ref):
        products = products_ref[...]
        start = pl.multiple_of((1 - core_ref[0]) * HALF, 128)
        theirs_ref[...] = plain_dot(buffer_ref[:, pl.ds(start, HALF)], products, (0, 0)).astype(bf16)
        gram_ref[...] = plain_dot(products, products, (0, 0))

    return pl.pallas_call(
        kernel,
        out_shape=(
            jax.ShapeDtypeStruct((RANK, RANK), f32),
            jax.ShapeDtypeStruct((HALF, RANK), bf16),
        ),
        in_specs=[SCALAR] + in_vmem(2),
        out_specs=tuple(in_vmem(2)),
        compiler_params=PARAMS,
    )(core, buffer, products)


def second_share(core, buffer, products):
    def kernel(core_ref, buffer_ref, products_ref, mine_ref):
        start = pl.multiple_of(core_ref[0] * HALF, 128)
        mine_ref[...] = plain_dot(buffer_ref[:, pl.ds(start, HALF)], products_ref[...], (0, 0))

    return pl.pallas_call(
        kernel,
        out_shape=jax.ShapeDtypeStruct((HALF, RANK), f32),
        in_specs=[SCALAR] + in_vmem(2),
        out_specs=in_vmem(1)[0],
        compiler_params=PARAMS,
    )(core, buffer, products)


def pack_shares(core, mine, theirs, gram, gram_other):
    def kernel(core_ref, mine_ref, theirs_ref, gram_ref, other_ref, out_ref):
        start = pl.multiple_of(core_ref[0] * (QUARTER // 2) + QUARTER, 8)
        energy = jnp.zeros((1, RANK), f32)
        size = jnp.zeros((1, RANK), f32)
        for i in range(PEERS):
            one = mine_ref[SHARE * i : SHARE * (i + 1), :]
            two = theirs_ref[SHARE * i : SHARE * (i + 1), :].astype(f32)
            both = one + two
            energy = energy + jnp.sum(one * one + two * two, axis=0, keepdims=True)
            size = size + jnp.sum(both * both, axis=0, keepdims=True)
            upper = slice(GRAM * i, GRAM * (i + 1))
            upper = gram_ref[upper, :QUARTER] + other_ref[upper, :QUARTER]
            lower = pl.ds(start + GRAM * (i // 2), GRAM)
            lower = gram_ref[lower, :] + other_ref[lower, :]
            lower = lower[4 * (i % 2) : 4 * (i % 2) + 4, :]
            lower = jnp.concatenate([lower[:, :QUARTER], lower[:, QUARTER:]], axis=0)
            parts = split(jnp.concatenate([upper, lower], axis=1))
            out_ref[i] = jnp.concatenate([both, *parts], axis=0).astype(bf16)
        growth = jnp.sum(energy / size, axis=1, keepdims=True) * (1.0 / RANK)

        @pl.when(jnp.logical_not(jnp.max(growth) <= LIMIT))
        def _():
            out_ref[...] = jnp.full(out_ref.shape, jnp.nan, bf16)

    return pl.pallas_call(
        kernel,
        out_shape=jax.ShapeDtypeStruct((PEERS, PACK, RANK), bf16),
        in_specs=[SCALAR] + in_vmem(4),
        out_specs=in_vmem(1)[0],
        compiler_params=PARAMS,
    )(core, mine, theirs, gram, gram_other)


def sum_shares(parts):
    def kernel(parts_ref, out_ref):
        total = jnp.zeros((PACK, RANK), f32)
        energy = jnp.zeros((1, RANK), f32)
        for i in range(PEERS):
            part = parts_ref[i].astype(f32)
            total = total + part
            energy = energy + jnp.sum(part[:SHARE] * part[:SHARE], axis=0, keepdims=True)
        total = guarded(total, energy, SHARE)
        gram = total[SHARE : SHARE + GRAM] + total[SHARE + GRAM :]
        packed = jnp.concatenate([total[:SHARE], *split(gram)], axis=0).astype(bf16)
        for i in range(PEERS):
            out_ref[i] = packed

    return pl.pallas_call(
        kernel,
        out_shape=jax.ShapeDtypeStruct(parts.shape, bf16),
        in_specs=in_vmem(1),
        out_specs=in_vmem(1)[0],
        compiler_params=PARAMS,
    )(parts)


def gram_block(ref, i):
    block = ref[i].astype(f32)
    return block[SHARE : SHARE + GRAM] + block[SHARE + GRAM :]


def second_moment(ref):
    full = TILES - 16
    rows = []
    keep = lax.broadcasted_iota(jnp.int32, (16, RANK), 0) < SHARE - full
    for i in range(PEERS):
        last = jnp.where(keep, ref[i, full:TILES, :].astype(f32), 0.0).astype(bf16)
        rows += [ref[i, :full, :], last]
    rows = jnp.concatenate(rows, axis=0)
    return plain_dot(rows, rows, (0, 0))


def diagonal(value):
    n = value.shape[0]
    rows = lax.broadcasted_iota(jnp.int32, (n, n), 0)
    cols = lax.broadcasted_iota(jnp.int32, (n, n), 1)
    return jnp.sum(jnp.where(rows == cols, value, 0.0), axis=0, keepdims=True)


def as_row(column):
    return diagonal(jnp.broadcast_to(column, (column.shape[0], column.shape[0])))


def first_factor(mine):
    def kernel(mine_ref, upper_ref, diagonal_ref, moment_ref):
        gram = jnp.concatenate(
            [gram_block(mine_ref, i)[:, :QUARTER] for i in range(PEERS)], axis=0
        )
        upper_ref[...] = triangle_inverse(gram, close_dot)
        diagonal_ref[...] = jnp.broadcast_to(diagonal(gram), (8, QUARTER))
        moment_ref[...] = second_moment(mine_ref)

    return pl.pallas_call(
        kernel,
        out_shape=(
            jax.ShapeDtypeStruct((QUARTER, QUARTER), f32),
            jax.ShapeDtypeStruct((8, QUARTER), f32),
            jax.ShapeDtypeStruct((RANK, RANK), f32),
        ),
        in_specs=in_vmem(1),
        out_specs=tuple(in_vmem(3)),
        compiler_params=PARAMS,
        cost_estimate=pl.CostEstimate(flops=10**10, bytes_accessed=10**6, transcendentals=0),
    )(mine)


def second_factor(core, mine, other, upper, diagonal_upper, moment):
    def kernel(
        core_ref, mine_ref, other_ref, upper_ref, diagonal_ref, moment_ref, high_ref, low_ref,
        stats_ref, rows_ref,
    ):
        for at, ref in enumerate((mine_ref, other_ref)):
            for i in range(PEERS):
                block = gram_block(ref, i)
                rows_ref[at, 4 * i : 4 * i + 4, :QUARTER] = block[:4, QUARTER:]
                rows_ref[at, 4 * i : 4 * i + 4, QUARTER:] = block[4:, QUARTER:]
        first = core_ref[0] == 0
        one, two = rows_ref[0], rows_ref[1]
        gram = jnp.concatenate([jnp.where(first, one, two), jnp.where(first, two, one)], axis=0)
        upper = upper_ref[...]
        below = close_dot(gram[:, :QUARTER], upper, (1, 1))
        rest = gram[:, QUARTER:]
        mixed = close_dot(below, upper, (1, 0))
        lower = triangle_inverse(rest - close_dot(below, below, (1, 1)), close_dot)
        corner = -close_dot(lower, mixed, (1, 0))
        zeros = jnp.zeros((QUARTER, QUARTER), f32)
        inverse = jnp.concatenate(
            [
                jnp.concatenate([upper, zeros], axis=1),
                jnp.concatenate([corner, lower], axis=1),
            ],
            axis=0,
        )
        scaled = math.sqrt(D) * inverse
        high = scaled.astype(bf16)
        high_ref[...] = high
        low_ref[...] = (scaled - high.astype(f32)).astype(bf16)
        moment = moment_ref[...] + second_moment(other_ref)
        low = low_ref[...]
        moment_high = moment.astype(bf16)
        moment_low = (moment - moment_high.astype(f32)).astype(bf16)
        product = plain_dot(high, moment_high, (1, 0)) + (
            plain_dot(high, moment_low, (1, 0)) + plain_dot(low, moment_high, (1, 0))
        )
        squares = as_row(jnp.sum(product * scaled, axis=1, keepdims=True))
        gram_diagonal = jnp.concatenate([diagonal_ref[0:1, :], diagonal(rest)], axis=1)
        weights = jnp.sum(inverse * inverse, axis=0, keepdims=True)
        growth = jnp.sum(gram_diagonal * weights, axis=1, keepdims=True) * (1.0 / RANK)
        noise = as_row(jnp.sum(scaled * scaled * diagonal(moment), axis=1, keepdims=True))
        ratio = jnp.where(squares > 0.0, noise / squares, jnp.inf)
        growth_cols = jnp.sum(ratio, axis=1, keepdims=True) * (1.0 / RANK)
        good = (growth <= LIMIT) & (growth_cols <= LIMIT)
        flag = jnp.broadcast_to(jnp.where(good, 0.0, 1.0), (1, RANK))
        stats = jnp.concatenate([squares, flag, jnp.zeros((6, RANK), f32)], axis=0)
        for i in range(DEPTHS):
            stats_ref[i] = stats

    square = jax.ShapeDtypeStruct((RANK, RANK), bf16)
    return pl.pallas_call(
        kernel,
        out_shape=(square, square, jax.ShapeDtypeStruct((DEPTHS, 8, RANK), f32)),
        in_specs=[SCALAR] + in_vmem(5),
        out_specs=tuple(in_vmem(3)),
        scratch_shapes=[pltpu.VMEM((2, QUARTER // 2, RANK), f32)],
        compiler_params=PARAMS,
    )(core, mine, other, upper, diagonal_upper, moment)


BLOCKS = ((0, 1664), (1664, 3328))
HBM = pl.BlockSpec(memory_space=pltpu.HBM)


def columns_and_momentum(core, mine, other, high, low, products, momentum, grad):
    def kernel(
        core_ref, mine_ref, other_ref, high_ref, low_ref, products_ref, momentum_hbm, grad_hbm,
        cols_ref, left_ref, new_hbm, momentum_ref, grad_ref, new_ref, sems,
    ):
        loads = []
        for i, (begin, end) in enumerate(BLOCKS):
            cut = pl.ds(begin, end - begin)
            two = (
                pltpu.make_async_copy(
                    momentum_hbm.at[:, cut], momentum_ref.at[:, cut], sems.at[0, i]
                ),
                pltpu.make_async_copy(grad_hbm.at[:, cut], grad_ref.at[:, cut], sems.at[1, i]),
            )
            for load in two:
                load.start()
            loads.append(two)
        high, low = high_ref[...], low_ref[...]
        products = products_ref[...]
        left = (plain_dot(products, high, (1, 1)) + plain_dot(products, low, (1, 1))).astype(bf16)
        left_ref[...] = left
        for ref, half in ((mine_ref, core_ref[0]), (other_ref, 1 - core_ref[0])):
            rows = jnp.concatenate([ref[i, :TILES, :] for i in range(PEERS)], axis=0)
            wide = plain_dot(rows, high, (1, 1)) + plain_dot(rows, low, (1, 1))
            for i in range(0, PEERS, 2):
                one = wide[TILES * i : TILES * i + SHARE, :]
                two = wide[TILES * (i + 1) : TILES * (i + 1) + SHARE, :]
                start = pl.multiple_of(half * HALF + SHARE * i, 16)
                pair = jnp.concatenate([one, two], axis=0).astype(bf16)
                cols_ref[pl.ds(start, 2 * SHARE), :] = pair
        copies = []
        for i, (begin, end) in enumerate(BLOCKS):
            cols = cols_ref[begin:end, :]
            for load in loads[i]:
                load.wait()
            buffer = (
                momentum_ref[:, begin:end].astype(f32) + grad_ref[:, begin:end].astype(f32)
            ).astype(bf16)
            new_ref[:, begin:end] = (
                buffer.astype(f32) - (1.0 - keep_rate) / D * plain_dot(left, cols, (1, 1))
            ).astype(bf16)
            cut = pl.ds(begin, end - begin)
            copy = pltpu.make_async_copy(new_ref.at[:, cut], new_hbm.at[:, cut], sems.at[2, i])
            copy.start()
            copies.append(copy)
        for copy in copies:
            copy.wait()

    return pl.pallas_call(
        kernel,
        out_shape=(
            jax.ShapeDtypeStruct((COLS, RANK), bf16),
            jax.ShapeDtypeStruct((ROWS, RANK), bf16),
            jax.ShapeDtypeStruct((ROWS, COLS), bf16),
        ),
        in_specs=[SCALAR] + in_vmem(5) + [HBM, HBM],
        out_specs=(*in_vmem(2), HBM),
        scratch_shapes=[
            pltpu.VMEM((ROWS, COLS), bf16),
            pltpu.VMEM((ROWS, COLS), bf16),
            pltpu.VMEM((ROWS, COLS), bf16),
            pltpu.SemaphoreType.DMA((3, len(BLOCKS))),
        ],
        compiler_params=PARAMS,
        cost_estimate=pl.CostEstimate(flops=5 * 10**9, bytes_accessed=10**6, transcendentals=0),
    )(core, mine, other, high, low, products, momentum, grad)


def factor_and_weight(stats, cols, left, weight):
    def kernel(
        stats_ref, cols_ref, left_ref, weight_hbm, factor_hbm, new_hbm, flag_ref,
        weight_ref, factor_ref, new_ref, sems, sem_factor,
    ):
        loads = []
        for i, (begin, end) in enumerate(BLOCKS):
            cut = pl.ds(begin, end - begin)
            load = pltpu.make_async_copy(
                weight_hbm.at[:, cut], weight_ref.at[:, cut], sems.at[0, i]
            )
            load.start()
            loads.append(load)
        total = stats_ref[0]
        for i in range(1, DEPTHS):
            total = total + stats_ref[i]
        inverse = lax.rsqrt(total[0:1, :] / FF + epsilon)
        flag_ref[0] = (jnp.max(total[1:2, :]) > 0.5).astype(jnp.int32)
        factor_ref[...] = (cols_ref[...].astype(f32) * inverse).astype(bf16)
        copies = [pltpu.make_async_copy(factor_ref, factor_hbm, sem_factor.at[0])]
        copies[0].start()
        left = left_ref[...]
        for i, (begin, end) in enumerate(BLOCKS):
            cut = pl.ds(begin, end - begin)
            loads[i].wait()
            new_ref[:, begin:end] = (
                weight_ref[:, begin:end].astype(f32)
                - step_rate / math.sqrt(RANK) * plain_dot(left, factor_ref[begin:end, :], (1, 1))
            ).astype(bf16)
            copy = pltpu.make_async_copy(new_ref.at[:, cut], new_hbm.at[:, cut], sems.at[1, i])
            copy.start()
            copies.append(copy)
        for copy in copies:
            copy.wait()

    return pl.pallas_call(
        kernel,
        out_shape=(
            jax.ShapeDtypeStruct((COLS, RANK), bf16),
            jax.ShapeDtypeStruct((ROWS, COLS), bf16),
            jax.ShapeDtypeStruct((1,), jnp.int32),
        ),
        in_specs=in_vmem(3) + [HBM],
        out_specs=(HBM, HBM, SCALAR),
        scratch_shapes=[
            pltpu.VMEM((ROWS, COLS), bf16),
            pltpu.VMEM((COLS, RANK), bf16),
            pltpu.VMEM((ROWS, COLS), bf16),
            pltpu.SemaphoreType.DMA((2, len(BLOCKS))),
            pltpu.SemaphoreType.DMA((1,)),
        ],
        compiler_params=PARAMS,
    )(stats, cols, left, weight)


def careful(weight, momentum, grad, q_factor):
    core = lax.axis_index(CORE)
    buffer = (momentum.astype(f32) + grad.astype(f32)).astype(bf16)
    partial_value = jnp.dot(buffer, q_factor, preferred_element_type=f32)
    products = gather(scatter_sum(partial_value, DEPTH, DEPTHS), DEPTH, DEPTHS)
    products = products.reshape(ROWS, RANK)
    gram = exact_dot(products, products, (0, 0))
    gram = gram + swap_core(gram)
    gram = gather(scatter_sum(gram, PLANE, PEERS), PLANE, PEERS).reshape(RANK, RANK)
    inverse = cholesky_inverse(gram)
    left_factor = (math.sqrt(D) * exact_dot(products, inverse, (1, 1))).astype(bf16)
    col_partial = plain_dot(buffer, left_factor, (0, 0))
    mine = lax.dynamic_slice_in_dim(col_partial, core * HALF, HALF, 0)
    theirs = lax.dynamic_slice_in_dim(col_partial, (1 - core) * HALF, HALF, 0)
    share = scatter_sum(mine + swap_core(theirs), PLANE, PEERS)
    squares = jnp.sum(gather(jnp.sum(share * share, axis=0)[None], EVERY, 256), axis=(0, 1))
    normalized = (share * lax.rsqrt(squares / FF + epsilon)).astype(bf16)
    mine = gather(normalized, PLANE, PEERS).reshape(HALF, RANK)
    new_factor = in_order(core, mine, swap_core(mine))
    scaled = (left_factor.astype(f32) * jnp.sqrt(squares / FF + epsilon)).astype(bf16)
    feedback = plain_dot(scaled, new_factor, (1, 1))
    new_momentum = (buffer.astype(f32) - (1.0 - keep_rate) / D * feedback).astype(bf16)
    update = plain_dot(left_factor, new_factor, (1, 1))
    new_weight = (weight.astype(f32) - step_rate / math.sqrt(RANK) * update).astype(bf16)
    return (new_weight, new_momentum, new_factor)


def on_device(weight, momentum, grad, q_factor):
    core = lax.axis_index(CORE).astype(jnp.int32).reshape(1)
    buffer, partial_value = buffer_and_products(momentum, grad, q_factor)
    core, partial_value = lax.optimization_barrier((core, partial_value))
    parts = exchange(partial_value.reshape(DEPTHS, ROWS // DEPTHS, RANK), DEPTH)
    products = exchange(sum_products(parts), DEPTH).reshape(ROWS, RANK)

    gram, theirs = first_shares(core, buffer, products)
    gram_other, theirs = swap_core(gram), swap_core(theirs)
    mine = second_share(core, buffer, products)
    parts = exchange(pack_shares(core, mine, theirs, gram, gram_other), PLANE)
    mine = exchange(sum_shares(parts), PLANE)
    other = swap_core(mine)
    upper, diagonal_upper, moment = first_factor(mine)
    high, low, stats = second_factor(core, mine, other, upper, diagonal_upper, moment)
    stats = exchange(stats, DEPTH)
    cols, left, new_momentum = columns_and_momentum(
        core, mine, other, high, low, products, momentum, grad
    )
    new_factor, new_weight, flag = factor_and_weight(stats, cols, left, weight)

    def again(state):
        return (jnp.zeros((1,), jnp.int32), *careful(weight, momentum, grad, q_factor))

    state = lax.while_loop(
        lambda state: state[0][0] > 0, again, (flag, new_weight, new_momentum, new_factor)
    )
    return state[1:]


def solution(mesh):
    fine = Mesh(mesh.devices.reshape(4, 4, 2, 8), EVERY)
    rows = ("x", "y", CORE)
    placed = (P(rows, DEPTH), P(rows, DEPTH), P(rows, DEPTH), P(DEPTH, None))
    return jax.shard_map(
        on_device,
        mesh=fine,
        in_specs=placed,
        out_specs=(P(rows, DEPTH), P(rows, DEPTH), P(DEPTH, None)),
        check_vma=False,
    )
```

```python
import math

import jax
import jax.numpy as jnp
from jax import lax
from jax.experimental import pallas as pl
from jax.experimental.pallas import tpu as pltpu
from jax.sharding import Mesh, PartitionSpec as P

D = 8192
FF = 26624
RANK = 256

epsilon = 1e-06
keep_rate = 0.9
step_rate = 0.5

HIGHEST = lax.Precision.HIGHEST
f32 = jnp.float32
bf16 = jnp.bfloat16

CORE = "core"
PLANE = ("x", "y")
DEPTH = "z"
COLUMN = ("core", "z")
EVERY = ("x", "y", "core", "z")

ROWS = 256
COLS = 3328
HALF = 1664
PEERS = 16
SHARE = 104
GRAM = 8
QUARTER = 128
PACK = 120
TILES = 112
DEPTHS = 8
PAIRS = 16
LIMIT = 4.0


def exact_dot(a, b, contract):
    dims = (((contract[0],), (contract[1],)), ((), ()))
    return lax.dot_general(a, b, dims, precision=HIGHEST, preferred_element_type=f32)


def plain_dot(a, b, contract):
    dims = (((contract[0],), (contract[1],)), ((), ()))
    return lax.dot_general(a, b, dims, preferred_element_type=f32)


def two_parts(value):
    high = value.astype(bf16)
    return high, (value - high.astype(f32)).astype(bf16)


def close_dot(a, b, contract):
    a_high, a_low = two_parts(a)
    b_high, b_low = two_parts(b)
    return plain_dot(a_high, b_high, contract) + (
        plain_dot(a_high, b_low, contract) + plain_dot(a_low, b_high, contract)
    )


def in_vmem(count):
    return [pl.BlockSpec(memory_space=pltpu.VMEM)] * count


SCALAR = pl.BlockSpec(memory_space=pltpu.SMEM)
PARAMS = pltpu.CompilerParams(vmem_limit_bytes=20 * 2**20)


LEAF = 64
PANEL = 16


def leaf_inverse(a):
    n = a.shape[0]
    lanes = 2 * n
    rows = lax.broadcasted_iota(jnp.int32, (n, n), 0)
    cols = lax.broadcasted_iota(jnp.int32, (n, n), 1)
    eye = (rows == cols).astype(f32)
    both = jnp.concatenate([a, eye], axis=1)
    count = n // 8
    slabs = [both[8 * i : 8 * i + 8, :] for i in range(count)]
    row8 = lax.broadcasted_iota(jnp.int32, (8, lanes), 0)
    for first in range(0, count, PANEL // 8):
        panel = [
            [
                jnp.broadcast_to(slabs[i][:, 8 * first + k : 8 * first + k + 1], (8, lanes))
                for i in range(first, count)
            ]
            for k in range(PANEL)
        ]
        for k in range(PANEL):
            at, sub = first + k // 8, k % 8
            pivot = jnp.broadcast_to(panel[k][at - first][sub : sub + 1, :], (8, lanes))
            inverse = 1.0 / pivot
            factor = {}
            for i in range(at, count):
                value = panel[k][i - first] * inverse
                factor[i] = jnp.where(row8 > sub, value, 0.0) if i == at else value
            for m in range(k + 1, PANEL):
                row = jnp.broadcast_to(panel[m][at - first][sub : sub + 1, :], (8, lanes))
                for i in range(at, count):
                    panel[m][i - first] = panel[m][i - first] - factor[i] * row
            row = jnp.broadcast_to(slabs[at][sub : sub + 1, :], (8, lanes))
            for i in range(at, count):
                slabs[i] = slabs[i] - factor[i] * row
    both = jnp.concatenate(slabs, axis=0)
    pivots = jnp.sum(both[:, :n] * eye, axis=1, keepdims=True)
    return both[:, n:] * lax.rsqrt(pivots)


def triangle_inverse(a, dot=exact_dot):
    n = a.shape[0]
    if n <= LEAF:
        return leaf_inverse(a)
    h = n // 2
    upper = triangle_inverse(a[:h, :h], dot)
    below = dot(a[h:, :h], upper, (1, 1))
    rest = a[h:, h:] - dot(below, below, (1, 1))
    mixed = dot(below, upper, (1, 0))
    lower = triangle_inverse(rest, dot)
    corner = -dot(lower, mixed, (1, 0))
    top = jnp.concatenate([upper, jnp.zeros((h, n - h), f32)], axis=1)
    return jnp.concatenate([top, jnp.concatenate([corner, lower], axis=1)], axis=0)


def cholesky_inverse(gram):
    def kernel(gram_ref, inverse_ref):
        inverse_ref[...] = triangle_inverse(gram_ref[...])

    return pl.pallas_call(
        kernel,
        out_shape=jax.ShapeDtypeStruct((RANK, RANK), f32),
        in_specs=in_vmem(1),
        out_specs=in_vmem(1)[0],
        compiler_params=PARAMS,
    )(gram)


def exchange(pieces, axis):
    return lax.all_to_all(pieces, axis, 0, 0)


def scatter_sum(value, axis, parts):
    pieces = value.reshape(parts, value.shape[0] // parts, *value.shape[1:])
    return jnp.sum(exchange(pieces, axis).astype(f32), axis=0)


def gather(value, axis, parts):
    return exchange(jnp.broadcast_to(value[None], (parts, *value.shape)), axis)


def swap_core(value):
    return lax.ppermute(value, CORE, [(0, 1), (1, 0)])


def in_order(core, mine, other):
    first = core == 0
    return jnp.concatenate([jnp.where(first, mine, other), jnp.where(first, other, mine)], axis=0)


def guarded(total, energy, rows):
    size = jnp.sum(total[:rows] * total[:rows], axis=0, keepdims=True)
    growth = jnp.sum(energy / size, axis=1, keepdims=True) * (1.0 / RANK)
    return jnp.where(growth <= LIMIT, total, jnp.nan)


def split(value):
    high = value.astype(bf16).astype(f32)
    return high, value - high


CUTS = (0, 896, 1792, 2560, 3328)


def buffer_and_products(momentum, grad, q_factor):
    def kernel(
        momentum_hbm, grad_hbm, q_hbm, buffer_ref, out_ref, momentum_ref, grad_ref, q_ref, sems
    ):
        copies = []
        for i, (low, high) in enumerate(zip(CUTS[:-1], CUTS[1:])):
            cut = pl.ds(low, high - low)
            three = (
                pltpu.make_async_copy(momentum_hbm.at[:, cut], momentum_ref.at[:, cut], sems.at[i, 0]),
                pltpu.make_async_copy(grad_hbm.at[:, cut], grad_ref.at[:, cut], sems.at[i, 1]),
                pltpu.make_async_copy(q_hbm.at[cut, :], q_ref.at[cut, :], sems.at[i, 2]),
            )
            for copy in three:
                copy.start()
            copies.append(three)
        total = jnp.zeros((ROWS, RANK), f32)
        for (low, high), three in zip(zip(CUTS[:-1], CUTS[1:]), copies):
            for copy in three:
                copy.wait()
            part = (
                momentum_ref[:, low:high].astype(f32) + grad_ref[:, low:high].astype(f32)
            ).astype(bf16)
            buffer_ref[:, low:high] = part
            total = total + plain_dot(part, q_ref[low:high, :], (1, 0))
        out_ref[...] = total.astype(bf16)

    return pl.pallas_call(
        kernel,
        out_shape=(
            jax.ShapeDtypeStruct((ROWS, COLS), bf16),
            jax.ShapeDtypeStruct((ROWS, RANK), bf16),
        ),
        in_specs=[pl.BlockSpec(memory_space=pltpu.HBM)] * 3,
        out_specs=tuple(in_vmem(2)),
        scratch_shapes=[
            pltpu.VMEM((ROWS, COLS), bf16),
            pltpu.VMEM((ROWS, COLS), bf16),
            pltpu.VMEM((COLS, RANK), bf16),
            pltpu.SemaphoreType.DMA((len(CUTS) - 1, 3)),
        ],
        compiler_params=PARAMS,
    )(momentum, grad, q_factor)


def sum_products(parts):
    def kernel(parts_ref, out_ref):
        total = jnp.zeros((ROWS // DEPTHS, RANK), f32)
        energy = jnp.zeros((1, RANK), f32)
        for i in range(DEPTHS):
            part = parts_ref[i].astype(f32)
            total = total + part
            energy = energy + jnp.sum(part * part, axis=0, keepdims=True)
        total = guarded(total, energy, ROWS // DEPTHS).astype(bf16)
        for i in range(DEPTHS):
            out_ref[i] = total

    return pl.pallas_call(
        kernel,
        out_shape=jax.ShapeDtypeStruct(parts.shape, bf16),
        in_specs=in_vmem(1),
        out_specs=in_vmem(1)[0],
        compiler_params=PARAMS,
    )(parts)


def first_shares(core, buffer, products):
    def kernel(core_ref, buffer_ref, products_ref, gram_ref, theirs_ref):
        products = products_ref[...]
        start = pl.multiple_of((1 - core_ref[0]) * HALF, 128)
        theirs_ref[...] = plain_dot(buffer_ref[:, pl.ds(start, HALF)], products, (0, 0)).astype(bf16)
        gram_ref[...] = plain_dot(products, products, (0, 0))

    return pl.pallas_call(
        kernel,
        out_shape=(
            jax.ShapeDtypeStruct((RANK, RANK), f32),
            jax.ShapeDtypeStruct((HALF, RANK), bf16),
        ),
        in_specs=[SCALAR] + in_vmem(2),
        out_specs=tuple(in_vmem(2)),
        compiler_params=PARAMS,
    )(core, buffer, products)


def second_share(core, buffer, products):
    def kernel(core_ref, buffer_ref, products_ref, mine_ref):
        start = pl.multiple_of(core_ref[0] * HALF, 128)
        mine_ref[...] = plain_dot(buffer_ref[:, pl.ds(start, HALF)], products_ref[...], (0, 0))

    return pl.pallas_call(
        kernel,
        out_shape=jax.ShapeDtypeStruct((HALF, RANK), f32),
        in_specs=[SCALAR] + in_vmem(2),
        out_specs=in_vmem(1)[0],
        compiler_params=PARAMS,
    )(core, buffer, products)


def pack_shares(core, mine, theirs, gram, gram_other):
    def kernel(core_ref, mine_ref, theirs_ref, gram_ref, other_ref, out_ref):
        start = pl.multiple_of(core_ref[0] * (QUARTER // 2) + QUARTER, 8)
        energy = jnp.zeros((1, RANK), f32)
        size = jnp.zeros((1, RANK), f32)
        for i in range(PEERS):
            one = mine_ref[SHARE * i : SHARE * (i + 1), :]
            two = theirs_ref[SHARE * i : SHARE * (i + 1), :].astype(f32)
            both = one + two
            energy = energy + jnp.sum(two * two, axis=0, keepdims=True)
            size = size + jnp.sum(both * both, axis=0, keepdims=True)
            upper = slice(GRAM * i, GRAM * (i + 1))
            upper = gram_ref[upper, :QUARTER] + other_ref[upper, :QUARTER]
            lower = pl.ds(start + GRAM * (i // 2), GRAM)
            lower = gram_ref[lower, :] + other_ref[lower, :]
            lower = lower[4 * (i % 2) : 4 * (i % 2) + 4, :]
            lower = jnp.concatenate([lower[:, :QUARTER], lower[:, QUARTER:]], axis=0)
            parts = split(jnp.concatenate([upper, lower], axis=1))
            out_ref[i] = jnp.concatenate([both, *parts], axis=0).astype(bf16)
        growth = jnp.sum(energy / size, axis=1, keepdims=True) * (1.0 / RANK)

        @pl.when(jnp.logical_not(jnp.max(growth) <= LIMIT))
        def _():
            out_ref[...] = jnp.full(out_ref.shape, jnp.nan, bf16)

    return pl.pallas_call(
        kernel,
        out_shape=jax.ShapeDtypeStruct((PEERS, PACK, RANK), bf16),
        in_specs=[SCALAR] + in_vmem(4),
        out_specs=in_vmem(1)[0],
        compiler_params=PARAMS,
    )(core, mine, theirs, gram, gram_other)


def sum_shares(parts):
    def kernel(parts_ref, out_ref):
        total = jnp.zeros((PACK, RANK), f32)
        energy = jnp.zeros((1, RANK), f32)
        for i in range(PEERS):
            part = parts_ref[i].astype(f32)
            total = total + part
            energy = energy + jnp.sum(part[:SHARE] * part[:SHARE], axis=0, keepdims=True)
        total = guarded(total, energy, SHARE)
        gram = total[SHARE : SHARE + GRAM] + total[SHARE + GRAM :]
        packed = jnp.concatenate([total[:SHARE], *split(gram)], axis=0).astype(bf16)
        for i in range(PEERS):
            out_ref[i] = packed

    return pl.pallas_call(
        kernel,
        out_shape=jax.ShapeDtypeStruct(parts.shape, bf16),
        in_specs=in_vmem(1),
        out_specs=in_vmem(1)[0],
        compiler_params=PARAMS,
    )(parts)


def gram_block(ref, i):
    block = ref[i].astype(f32)
    return block[SHARE : SHARE + GRAM] + block[SHARE + GRAM :]


def second_moment(ref):
    full = TILES - 16
    rows = []
    keep = lax.broadcasted_iota(jnp.int32, (16, RANK), 0) < SHARE - full
    for i in range(PEERS):
        last = jnp.where(keep, ref[i, full:TILES, :].astype(f32), 0.0).astype(bf16)
        rows += [ref[i, :full, :], last]
    rows = jnp.concatenate(rows, axis=0)
    return plain_dot(rows, rows, (0, 0))


def diagonal(value):
    n = value.shape[0]
    rows = lax.broadcasted_iota(jnp.int32, (n, n), 0)
    cols = lax.broadcasted_iota(jnp.int32, (n, n), 1)
    return jnp.sum(jnp.where(rows == cols, value, 0.0), axis=0, keepdims=True)


def as_row(column):
    return diagonal(jnp.broadcast_to(column, (column.shape[0], column.shape[0])))


def first_factor(mine):
    def kernel(mine_ref, upper_ref, diagonal_ref, moment_ref):
        gram = jnp.concatenate(
            [gram_block(mine_ref, i)[:, :QUARTER] for i in range(PEERS)], axis=0
        )
        upper_ref[...] = triangle_inverse(gram, close_dot)
        diagonal_ref[...] = jnp.broadcast_to(diagonal(gram), (8, QUARTER))
        moment_ref[...] = second_moment(mine_ref)

    return pl.pallas_call(
        kernel,
        out_shape=(
            jax.ShapeDtypeStruct((QUARTER, QUARTER), f32),
            jax.ShapeDtypeStruct((8, QUARTER), f32),
            jax.ShapeDtypeStruct((RANK, RANK), f32),
        ),
        in_specs=in_vmem(1),
        out_specs=tuple(in_vmem(3)),
        compiler_params=PARAMS,
        cost_estimate=pl.CostEstimate(flops=10**10, bytes_accessed=10**6, transcendentals=0),
    )(mine)


def second_factor(core, mine, other, upper, diagonal_upper, moment):
    def kernel(
        core_ref, mine_ref, other_ref, upper_ref, diagonal_ref, moment_ref, high_ref, low_ref,
        stats_ref, rows_ref,
    ):
        for at, ref in enumerate((mine_ref, other_ref)):
            for i in range(PEERS):
                block = gram_block(ref, i)
                rows_ref[at, 4 * i : 4 * i + 4, :QUARTER] = block[:4, QUARTER:]
                rows_ref[at, 4 * i : 4 * i + 4, QUARTER:] = block[4:, QUARTER:]
        first = core_ref[0] == 0
        one, two = rows_ref[0], rows_ref[1]
        gram = jnp.concatenate([jnp.where(first, one, two), jnp.where(first, two, one)], axis=0)
        upper = upper_ref[...]
        below = close_dot(gram[:, :QUARTER], upper, (1, 1))
        rest = gram[:, QUARTER:]
        mixed = close_dot(below, upper, (1, 0))
        lower = triangle_inverse(rest - close_dot(below, below, (1, 1)), close_dot)
        corner = -close_dot(lower, mixed, (1, 0))
        zeros = jnp.zeros((QUARTER, QUARTER), f32)
        inverse = jnp.concatenate(
            [
                jnp.concatenate([upper, zeros], axis=1),
                jnp.concatenate([corner, lower], axis=1),
            ],
            axis=0,
        )
        scaled = math.sqrt(D) * inverse
        high = scaled.astype(bf16)
        high_ref[...] = high
        low_ref[...] = (scaled - high.astype(f32)).astype(bf16)
        moment = moment_ref[...]
        low = low_ref[...]
        moment_high = moment.astype(bf16)
        moment_low = (moment - moment_high.astype(f32)).astype(bf16)
        product = plain_dot(high, moment_high, (1, 0)) + (
            plain_dot(high, moment_low, (1, 0)) + plain_dot(low, moment_high, (1, 0))
        )
        squares = as_row(jnp.sum(product * scaled, axis=1, keepdims=True))
        gram_diagonal = jnp.concatenate([diagonal_ref[0:1, :], diagonal(rest)], axis=1)
        weights = jnp.sum(inverse * inverse, axis=0, keepdims=True)
        growth = jnp.sum(gram_diagonal * weights, axis=1, keepdims=True) * (1.0 / RANK)
        noise = as_row(jnp.sum(scaled * scaled * diagonal(moment), axis=1, keepdims=True))
        ratio = jnp.where(squares > 0.0, noise / squares, jnp.inf)
        growth_cols = jnp.sum(ratio, axis=1, keepdims=True) * (1.0 / RANK)
        good = (growth <= LIMIT) & (growth_cols <= LIMIT)
        flag = jnp.broadcast_to(jnp.where(good, 0.0, 1.0), (1, RANK))
        stats = jnp.concatenate([squares, flag, jnp.zeros((6, RANK), f32)], axis=0)
        for i in range(PAIRS):
            stats_ref[i] = stats

    square = jax.ShapeDtypeStruct((RANK, RANK), bf16)
    return pl.pallas_call(
        kernel,
        out_shape=(square, square, jax.ShapeDtypeStruct((PAIRS, 8, RANK), f32)),
        in_specs=[SCALAR] + in_vmem(5),
        out_specs=tuple(in_vmem(3)),
        scratch_shapes=[pltpu.VMEM((2, QUARTER // 2, RANK), f32)],
        compiler_params=PARAMS,
    )(core, mine, other, upper, diagonal_upper, moment)


BLOCKS = ((0, 1664), (1664, 3328))
HBM = pl.BlockSpec(memory_space=pltpu.HBM)


def columns_and_momentum(core, mine, other, high, low, products, momentum, grad):
    def kernel(
        core_ref, mine_ref, other_ref, high_ref, low_ref, products_ref, momentum_hbm, grad_hbm,
        cols_ref, left_ref, new_hbm, momentum_ref, grad_ref, new_ref, sems,
    ):
        loads = []
        for i, (begin, end) in enumerate(BLOCKS):
            cut = pl.ds(begin, end - begin)
            two = (
                pltpu.make_async_copy(
                    momentum_hbm.at[:, cut], momentum_ref.at[:, cut], sems.at[0, i]
                ),
                pltpu.make_async_copy(grad_hbm.at[:, cut], grad_ref.at[:, cut], sems.at[1, i]),
            )
            for load in two:
                load.start()
            loads.append(two)
        high, low = high_ref[...], low_ref[...]
        products = products_ref[...]
        left = (plain_dot(products, high, (1, 1)) + plain_dot(products, low, (1, 1))).astype(bf16)
        left_ref[...] = left
        for ref, half in ((mine_ref, core_ref[0]), (other_ref, 1 - core_ref[0])):
            rows = jnp.concatenate([ref[i, :TILES, :] for i in range(PEERS)], axis=0)
            wide = plain_dot(rows, high, (1, 1)) + plain_dot(rows, low, (1, 1))
            for i in range(0, PEERS, 2):
                one = wide[TILES * i : TILES * i + SHARE, :]
                two = wide[TILES * (i + 1) : TILES * (i + 1) + SHARE, :]
                start = pl.multiple_of(half * HALF + SHARE * i, 16)
                pair = jnp.concatenate([one, two], axis=0).astype(bf16)
                cols_ref[pl.ds(start, 2 * SHARE), :] = pair
        copies = []
        for i, (begin, end) in enumerate(BLOCKS):
            cols = cols_ref[begin:end, :]
            for load in loads[i]:
                load.wait()
            buffer = (
                momentum_ref[:, begin:end].astype(f32) + grad_ref[:, begin:end].astype(f32)
            ).astype(bf16)
            new_ref[:, begin:end] = (
                buffer.astype(f32) - (1.0 - keep_rate) / D * plain_dot(left, cols, (1, 1))
            ).astype(bf16)
            cut = pl.ds(begin, end - begin)
            copy = pltpu.make_async_copy(new_ref.at[:, cut], new_hbm.at[:, cut], sems.at[2, i])
            copy.start()
            copies.append(copy)
        for copy in copies:
            copy.wait()

    return pl.pallas_call(
        kernel,
        out_shape=(
            jax.ShapeDtypeStruct((COLS, RANK), bf16),
            jax.ShapeDtypeStruct((ROWS, RANK), bf16),
            jax.ShapeDtypeStruct((ROWS, COLS), bf16),
        ),
        in_specs=[SCALAR] + in_vmem(5) + [HBM, HBM],
        out_specs=(*in_vmem(2), HBM),
        scratch_shapes=[
            pltpu.VMEM((ROWS, COLS), bf16),
            pltpu.VMEM((ROWS, COLS), bf16),
            pltpu.VMEM((ROWS, COLS), bf16),
            pltpu.SemaphoreType.DMA((3, len(BLOCKS))),
        ],
        compiler_params=PARAMS,
        cost_estimate=pl.CostEstimate(flops=5 * 10**9, bytes_accessed=10**6, transcendentals=0),
    )(core, mine, other, high, low, products, momentum, grad)


def factor_and_weight(stats, cols, left, weight):
    def kernel(
        stats_ref, cols_ref, left_ref, weight_hbm, factor_hbm, new_hbm, flag_ref,
        weight_ref, factor_ref, new_ref, sems, sem_factor,
    ):
        loads = []
        for i, (begin, end) in enumerate(BLOCKS):
            cut = pl.ds(begin, end - begin)
            load = pltpu.make_async_copy(
                weight_hbm.at[:, cut], weight_ref.at[:, cut], sems.at[0, i]
            )
            load.start()
            loads.append(load)
        total = stats_ref[0]
        for i in range(1, PAIRS):
            total = total + stats_ref[i]
        inverse = lax.rsqrt(total[0:1, :] / FF + epsilon)
        flag_ref[0] = (jnp.max(total[1:2, :]) > 0.5).astype(jnp.int32)
        factor_ref[...] = (cols_ref[...].astype(f32) * inverse).astype(bf16)
        copies = [pltpu.make_async_copy(factor_ref, factor_hbm, sem_factor.at[0])]
        copies[0].start()
        left = left_ref[...]
        for i, (begin, end) in enumerate(BLOCKS):
            cut = pl.ds(begin, end - begin)
            loads[i].wait()
            new_ref[:, begin:end] = (
                weight_ref[:, begin:end].astype(f32)
                - step_rate / math.sqrt(RANK) * plain_dot(left, factor_ref[begin:end, :], (1, 1))
            ).astype(bf16)
            copy = pltpu.make_async_copy(new_ref.at[:, cut], new_hbm.at[:, cut], sems.at[1, i])
            copy.start()
            copies.append(copy)
        for copy in copies:
            copy.wait()

    return pl.pallas_call(
        kernel,
        out_shape=(
            jax.ShapeDtypeStruct((COLS, RANK), bf16),
            jax.ShapeDtypeStruct((ROWS, COLS), bf16),
            jax.ShapeDtypeStruct((1,), jnp.int32),
        ),
        in_specs=in_vmem(3) + [HBM],
        out_specs=(HBM, HBM, SCALAR),
        scratch_shapes=[
            pltpu.VMEM((ROWS, COLS), bf16),
            pltpu.VMEM((COLS, RANK), bf16),
            pltpu.VMEM((ROWS, COLS), bf16),
            pltpu.SemaphoreType.DMA((2, len(BLOCKS))),
            pltpu.SemaphoreType.DMA((1,)),
        ],
        compiler_params=PARAMS,
    )(stats, cols, left, weight)


def careful(weight, momentum, grad, q_factor):
    core = lax.axis_index(CORE)
    buffer = (momentum.astype(f32) + grad.astype(f32)).astype(bf16)
    partial_value = jnp.dot(buffer, q_factor, preferred_element_type=f32)
    products = gather(scatter_sum(partial_value, DEPTH, DEPTHS), DEPTH, DEPTHS)
    products = products.reshape(ROWS, RANK)
    gram = exact_dot(products, products, (0, 0))
    gram = gram + swap_core(gram)
    gram = gather(scatter_sum(gram, PLANE, PEERS), PLANE, PEERS).reshape(RANK, RANK)
    inverse = cholesky_inverse(gram)
    left_factor = (math.sqrt(D) * exact_dot(products, inverse, (1, 1))).astype(bf16)
    col_partial = plain_dot(buffer, left_factor, (0, 0))
    mine = lax.dynamic_slice_in_dim(col_partial, core * HALF, HALF, 0)
    theirs = lax.dynamic_slice_in_dim(col_partial, (1 - core) * HALF, HALF, 0)
    share = scatter_sum(mine + swap_core(theirs), PLANE, PEERS)
    squares = jnp.sum(gather(jnp.sum(share * share, axis=0)[None], EVERY, 256), axis=(0, 1))
    normalized = (share * lax.rsqrt(squares / FF + epsilon)).astype(bf16)
    mine = gather(normalized, PLANE, PEERS).reshape(HALF, RANK)
    new_factor = in_order(core, mine, swap_core(mine))
    scaled = (left_factor.astype(f32) * jnp.sqrt(squares / FF + epsilon)).astype(bf16)
    feedback = plain_dot(scaled, new_factor, (1, 1))
    new_momentum = (buffer.astype(f32) - (1.0 - keep_rate) / D * feedback).astype(bf16)
    update = plain_dot(left_factor, new_factor, (1, 1))
    new_weight = (weight.astype(f32) - step_rate / math.sqrt(RANK) * update).astype(bf16)
    return (new_weight, new_momentum, new_factor)


def on_device(weight, momentum, grad, q_factor):
    core = lax.axis_index(CORE).astype(jnp.int32).reshape(1)
    buffer, partial_value = buffer_and_products(momentum, grad, q_factor)
    core, partial_value = lax.optimization_barrier((core, partial_value))
    parts = exchange(partial_value.reshape(DEPTHS, ROWS // DEPTHS, RANK), DEPTH)
    products = exchange(sum_products(parts), DEPTH).reshape(ROWS, RANK)

    gram, theirs = first_shares(core, buffer, products)
    gram_other, theirs = swap_core(gram), swap_core(theirs)
    mine = second_share(core, buffer, products)
    parts = exchange(pack_shares(core, mine, theirs, gram, gram_other), PLANE)
    mine = exchange(sum_shares(parts), PLANE)
    other = swap_core(mine)
    upper, diagonal_upper, moment = first_factor(mine)
    high, low, stats = second_factor(core, mine, other, upper, diagonal_upper, moment)
    stats = exchange(stats, COLUMN)
    cols, left, new_momentum = columns_and_momentum(
        core, mine, other, high, low, products, momentum, grad
    )
    new_factor, new_weight, flag = factor_and_weight(stats, cols, left, weight)

    def again(state):
        return (jnp.zeros((1,), jnp.int32), *careful(weight, momentum, grad, q_factor))

    state = lax.while_loop(
        lambda state: state[0][0] > 0, again, (flag, new_weight, new_momentum, new_factor)
    )
    return state[1:]


def solution(mesh):
    fine = Mesh(mesh.devices.reshape(4, 4, 2, 8), EVERY)
    rows = ("x", "y", CORE)
    placed = (P(rows, DEPTH), P(rows, DEPTH), P(rows, DEPTH), P(DEPTH, None))
    return jax.shard_map(
        on_device,
        mesh=fine,
        in_specs=placed,
        out_specs=(P(rows, DEPTH), P(rows, DEPTH), P(DEPTH, None)),
        check_vma=False,
    )
```
